512 devices in a mesh: seq: 8 (over y, core), head: 64 (over z, x).
Axes of the slice: x: 4, y: 4, z: 16, core: 2. Of those that a mesh axis runs over, the one named last changes fastest.
Arguments:
- tokens: bfloat16 [8192, 2048], P('seq', 'head'), may hold values from -6 to 6
- z_weight: bfloat16 [2048, 4096], P(None, 'head'), may hold values from -0.125 to 0.125
- x_weight: bfloat16 [2048, 4096], P(None, 'head'), may hold values from -0.79549513 to 0.79549513
- bc_weight: bfloat16 [2048, 256], replicated, may hold values from -0.125 to 0.125
- step_weight: bfloat16 [2048, 64], P(None, 'head'), may hold values from -0.125 to 0.125
- x_kernel: float32 [4, 4096], P(None, 'head'), may hold values from -3 to 3
- bc_kernel: float32 [4, 256], replicated, may hold values from -3 to 3
- step_bias: float32 [64], P('head'), may hold values from -9 to -3
- log_decay: float32 [64], P('head'), may hold values from 0 to 1.5
- skip_gain: float32 [64], P('head'), may hold values from 0.2 to 0.8
- norm_gain: bfloat16 [4096], P('head'), may hold values from 0.099609375 to 1.8984375
- out_weight: bfloat16 [4096, 2048], P('head'), may hold values from -0.09375 to 0.09375
Outputs:
- mixed: bfloat16 [8192, 2048], P('seq', 'head')
The draws below stay inside these ranges and needn't reach their ends.
All inputs are finite; a program needn't handle non-finite values.
Results may differ from the reference program's by a relative error of at most 0.017.
Values may be sent and summed in bfloat16 or wider, within the bound.
A program may use at most 64 MiB of HBM per device.

```python
import jax
import jax.numpy as jnp
from jax import lax

D = 2048
HEADS = 64
P_SIZE = 64
N = 128
CH = 256
E = 4096
TOKENS = 8192


def draw_x_weight(key, part):
    key = jax.random.fold_in(key, 11)
    base = jax.random.truncated_normal(key, -4.0, 4.0, (D, HEADS * P_SIZE), jnp.float32)
    position = (jnp.arange(HEADS * P_SIZE) // P_SIZE).astype(jnp.float32) / (HEADS - 1)
    ratio = 3.0
    return (base * D ** (-0.5) * jnp.power(ratio, position)[None, :]).astype(jnp.bfloat16)


def draw_step_bias(key, part):
    key = jax.random.fold_in(key, 23)
    result = jax.random.uniform(key, (HEADS,), jnp.float32, -8.5, -3.0)
    return result


def block_scale(key, extent, pieces, least, top_value):
    factor_of = 1.0
    for dim, parts in pieces:
        draws = jax.random.uniform(jax.random.fold_in(jax.random.fold_in(key, 6), dim), (parts,), jnp.float32, least / len(pieces), top_value / len(pieces))
        factor_of = factor_of * jnp.repeat(jnp.exp(draws), extent[dim] // parts).reshape((-1,) + (1,) * (len(extent) - 1 - dim))
    return factor_of


def scatter_about(rng, extent, scale, bound, pieces=(), kind=jnp.bfloat16):
    values = jax.random.normal(rng, extent, jnp.float32) * scale
    if len(pieces) > 0:
        values = block_scale(rng, extent, pieces, -0.22, 0.18) * values
    return jnp.clip(values, min=-bound, max=bound).astype(kind)


def setup_inputs(seed: int = 0) -> dict:
    arg_keys = jax.random.split(jax.random.key(seed), 13)
    return {
        "tokens": scatter_about(arg_keys[0], (TOKENS, D), 1.0, 6.0, ((0, 8), (1, 64))),
        "z_weight": scatter_about(arg_keys[1], (D, E), D ** -0.5, 0.125, ((1, 64),)),
        "x_weight": draw_x_weight(jax.random.fold_in(arg_keys[12], 71), 0),
        "bc_weight": scatter_about(arg_keys[3], (D, 2 * N), D ** -0.5, 0.125),
        "step_weight": scatter_about(arg_keys[4], (D, HEADS), D ** -0.5, 0.125, ((1, 64),)),
        "x_kernel": scatter_about(arg_keys[5], (4, E), 4 ** -0.5, 3.0, ((1, 64),), jnp.float32),
        "bc_kernel": scatter_about(arg_keys[6], (4, 2 * N), 4 ** -0.5, 3.0, (), jnp.float32),
        "step_bias": draw_step_bias(jax.random.fold_in(arg_keys[12], 71), 0),
        "log_decay": jnp.clip(1.5 * jax.random.uniform(arg_keys[8], (HEADS,), jnp.float32) ** block_scale(arg_keys[8], (HEADS,), ((0, 64),), -0.2, 0.2), 0.0, 1.5),
        "skip_gain": jnp.clip(0.2 + 0.6 * jax.random.uniform(arg_keys[9], (HEADS,), jnp.float32) ** block_scale(arg_keys[9], (HEADS,), ((0, 64),), -0.2, 0.2), 0.2, 0.8),
        "norm_gain": jnp.clip(1.0 + 0.18 * jax.random.normal(arg_keys[10], (E,), jnp.float32), 0.099609375, 1.8984375).astype(jnp.bfloat16),
        "out_weight": scatter_about(arg_keys[11], (E, D), E ** -0.5, 0.09375, ((0, 64),)),
    }


def causal(padded, kernel):
    length = padded.shape[0] - 3
    total = kernel[0] * padded[0:length].astype(jnp.float32)
    for offset in range(1, 4):
        total = total + kernel[offset] * padded[offset:offset + length].astype(jnp.float32)
    return jax.nn.silu(total).astype(jnp.bfloat16)

def reference(tokens, z_weight, x_weight, bc_weight, step_weight, x_kernel, bc_kernel, step_bias, log_decay, skip_gain, norm_gain, out_weight):
    z_in = jnp.dot(tokens, z_weight, preferred_element_type=jnp.float32).astype(jnp.bfloat16)
    x_in = jnp.dot(tokens, x_weight, preferred_element_type=jnp.float32).astype(jnp.bfloat16)
    bc_in = jnp.dot(tokens, bc_weight, preferred_element_type=jnp.float32).astype(jnp.bfloat16)
    step_raw = jnp.dot(tokens, step_weight, preferred_element_type=jnp.float32)
    x_conv = causal(jnp.concatenate([jnp.zeros((3, x_in.shape[1]), x_in.dtype), x_in], axis=0), x_kernel)
    bc_conv = causal(jnp.concatenate([jnp.zeros((3, bc_in.shape[1]), bc_in.dtype), bc_in], axis=0), bc_kernel)
    blocks = TOKENS // CH
    b_map = bc_conv[:, :N].reshape(blocks, CH, N)
    c_map = bc_conv[:, N:].reshape(blocks, CH, N)
    step_size = jax.nn.softplus(step_raw + step_bias)
    rate = -jnp.exp(log_decay) * step_size
    values = x_conv.reshape(blocks, CH, HEADS, P_SIZE)
    steps_b = step_size.reshape(blocks, CH, HEADS)
    cumulative = jnp.cumsum(rate.reshape(blocks, CH, HEADS), axis=1)
    lower = (jnp.arange(CH)[:, None] >= jnp.arange(CH)[None, :])[None, :, :, None]
    gram = jnp.einsum('ctn,csn->cts', c_map.astype(jnp.float32), b_map.astype(jnp.float32))
    spread = cumulative[:, :, None, :] - cumulative[:, None, :, :]
    mixing = jnp.where(lower, gram[..., None] * jnp.exp(jnp.where(lower, spread, 0.0)) * steps_b[:, None, :, :], 0.0).astype(jnp.bfloat16)
    intra = jnp.einsum('ctsh,cshp->cthp', mixing.astype(jnp.float32), values.astype(jnp.float32))
    tails = jnp.exp(cumulative[:, -1:, :] - cumulative) * steps_b
    weighted = (values.astype(jnp.float32) * tails[..., None]).astype(jnp.bfloat16)
    local = jnp.einsum('cthp,ctn->chpn', weighted.astype(jnp.float32), b_map.astype(jnp.float32))
    block_decay = jnp.exp(cumulative[:, -1, :])

    def advance(state, item):
        term, decay = item
        return (decay[:, None, None] * state + term, state)
    start_state = jnp.zeros((HEADS, P_SIZE, N), jnp.float32)
    last_state, entering = lax.scan(advance, start_state, (local, block_decay))
    held = entering.astype(jnp.bfloat16)
    from_state = jnp.einsum('ctn,chpn->cthp', c_map.astype(jnp.float32), held.astype(jnp.float32)) * jnp.exp(cumulative)[..., None]
    output_y = intra + from_state + skip_gain[None, None, :, None] * values.astype(jnp.float32)
    gated = (output_y.reshape(TOKENS, HEADS * P_SIZE) * jax.nn.silu(z_in.astype(jnp.float32))).astype(jnp.bfloat16)
    gated_f = gated.astype(jnp.float32)
    meansq = lax.optimization_barrier(jnp.mean(gated_f * gated_f, axis=1))
    scaled = (gated_f * norm_gain.astype(jnp.float32)).astype(jnp.bfloat16)
    projected = jnp.dot(scaled, out_weight, preferred_element_type=jnp.float32)
    return (projected * lax.rsqrt(meansq + 1e-05)[:, None]).astype(jnp.bfloat16)
```

```python
import functools

import jax
import jax.numpy as jnp
from jax import lax
from jax.experimental import pallas as pl
from jax.experimental.pallas import tpu as pltpu
from jax.sharding import PartitionSpec as P

MESH = pl.DeviceIdType.MESH
F32 = jnp.float32
BF16 = jnp.bfloat16
NX = 4
BLK = 256
NONE = (((1,), (0,)), ((), ()))
BOTH = (((1,), (1,)), ((), ()))


def dot(a, b, dims=NONE):
    return lax.dot_general(a, b, dims, preferred_element_type=F32)


def kernel(
    ns,
    nz,
    tok_in,
    zw_in,
    xw_in,
    bcw_in,
    sw_in,
    xk_in,
    bck_in,
    bias_in,
    decay_in,
    skip_in,
    gain_in,
    ow_in,
    out_ref,
    tok,
    zw,
    xw,
    bcw,
    bct,
    ow,
    owt,
    par,
    swf,
    pt,
    ptt,
    ct,
    xin,
    zsil,
    xc,
    halo_s,
    halo_r,
    tr,
    bcv,
    wt,
    yv,
    st1s,
    st1r,
    st2s,
    st2r,
    hs,
    held,
    sqs,
    sqr,
    sc,
    rs_rs,
    rs_ls,
    rs_rr,
    rs_lr,
    res,
    lsem,
    p1s,
    p1r,
    ws,
    wr,
    sibs,
    sibr,
    ps,
    pr,
    ags,
    agr,
    hsem,
    s1s,
    s1r,
    s2s,
    s2r,
    s3s,
    s3r,
    sqss,
    sqrs,
    rss,
    rsr,
    p4s,
    p4r,
):
    half = nz // 2
    width = 128 * nz
    s = lax.axis_index("seq")
    h = lax.axis_index("head")
    z = h // NX
    x = lax.rem(h, NX)
    core = lax.rem(s, 2)
    block = s * NX + x
    blocks = ns * NX

    def at(s_to, z_to, x_to):
        return (s_to, z_to * NX + x_to)

    def mod(v, n):
        return lax.rem(v + n, n)

    right = at(s, mod(z + 1, nz), x)
    left = at(s, mod(z - 1, nz), x)
    x_up = at(s, z, mod(x + 1, NX))
    x_down = at(s, z, mod(x - 1, NX))
    sibling = (s + 1 - 2 * core, h)
    after = mod(block + 1, blocks)
    before = mod(block - 1, blocks)
    next_dev = at(after // NX, z, lax.rem(after, NX))
    prev_dev = at(before // NX, z, lax.rem(before, NX))

    def remote(src, dst, send, recv, to):
        return pltpu.make_async_remote_copy(
            src_ref=src, dst_ref=dst, send_sem=send, recv_sem=recv, device_id=to, device_id_type=MESH
        )

    def rows(ref, start, count):
        return ref.at[pl.ds(pl.multiple_of(start, count), count)]

    own_tok = rows(tok, 128 * z + 32 * x, 32)
    my_cols = pl.ds(pl.multiple_of(BLK * x, BLK), BLK)
    local = [
        pltpu.make_async_copy(tok_in.at[:, my_cols], own_tok, lsem.at[0]),
        pltpu.make_async_copy(bcw_in, bcw, lsem.at[1]),
        pltpu.make_async_copy(zw_in, rows(zw, 64 * x, 64), lsem.at[2]),
        pltpu.make_async_copy(xw_in, rows(xw, 64 * x, 64), lsem.at[3]),
        pltpu.make_async_copy(ow_in, rows(ow, 64 * x, 64), lsem.at[4]),
    ]
    for c in local:
        c.start()

    barrier = pltpu.get_barrier_semaphore()

    def greet(to):
        pl.semaphore_signal(barrier, inc=1, device_id=to, device_id_type=MESH)

    for d in range(1, NX):
        greet(at(s, z, mod(x + d, NX)))
    for d in range(1, nz):
        greet(at(s, mod(z + d, nz), x))
    for d in range(1, ns):
        greet((mod(s + d, ns), h))
    greet(next_dev)
    greet(prev_dev)

    par[x] = jnp.zeros((24, 128), F32)
    sw = sw_in[...].astype(F32)
    for r in range(nz):
        par[x, r : r + 1, :] = sw[:, 128 * r : 128 * r + 128]
    xk = xk_in[...]
    par[x, 16:20, :] = jnp.concatenate([xk, xk], axis=1)
    gain = gain_in[...].astype(F32)
    par[x, 20:21, :] = jnp.concatenate([gain, gain], axis=1)
    par[x, 21:22, :] = jnp.full((1, 128), bias_in[0], F32)
    par[x, 22:23, :] = jnp.full((1, 128), decay_in[0], F32)
    par[x, 23:24, :] = jnp.full((1, 128), skip_in[0], F32)

    pl.semaphore_wait(barrier, (NX - 1) + (nz - 1) + (ns - 1) + 2)

    p1 = []
    for d in range(1, NX):
        xp = mod(x + d, NX)
        cols = pl.ds(pl.multiple_of(BLK * xp, BLK), BLK)
        c = remote(tok_in.at[:, cols], own_tok, p1s.at[d - 1], p1r.at[d - 1], at(s, z, xp))
        c.start()
        p1.append(c)
    small = []
    for d in range(1, NX):
        c = remote(par.at[x], par.at[x], ps.at[d - 1], pr.at[d - 1], at(s, z, mod(x + d, NX)))
        c.start()
        small.append(c)

    hr = 32 * core

    def wrow(ref, j):
        return rows(ref, 64 * j + hr, 32)

    half_in = pl.ds(pl.multiple_of(hr, 32), 32)
    wx = []
    for n, (src, buf) in enumerate(((zw_in, zw), (xw_in, xw))):
        up = remote(src.at[half_in], wrow(buf, x), ws.at[2 * n], wr.at[2 * n], x_up)
        down = remote(src.at[half_in], wrow(buf, x), ws.at[2 * n + 1], wr.at[2 * n + 1], x_down)
        wx.append((up, down))

    for c in local:
        c.wait()
    for c in p1:
        c.wait_recv()
    wx[1][0].start()
    wx[0][1].start()
    wx[0][0].start()
    wx[1][1].start()

    def ag(k, p, direction):
        src = mod(z - k, nz) if direction == 0 else mod(z + k, nz)
        ref = rows(tok, 128 * src + 64 * p, 64)
        to = right if direction == 0 else left
        return remote(ref, ref, ags.at[direction, k, p], agr.at[direction, k, p], to)

    def ag_wait(k, p, direction):
        src = mod(z - k - 1, nz) if direction == 0 else mod(z + k + 1, nz)
        ref = rows(tok, 128 * src + 64 * p, 64)
        remote(ref, ref, ags.at[direction, k, p], agr.at[direction, k, p], right).wait_recv()

    def transpose_bc(k):
        piece = bcw[pl.ds(pl.multiple_of(BLK * k, BLK), BLK), :]
        bct[:, pl.ds(pl.multiple_of(BLK * k, BLK), BLK)] = piece.T

    for p in range(2):
        for direction in range(2):
            ag(0, p, direction).start()
    transpose_bc(0)

    def ag_step(k, _):
        for p in range(2):
            for direction in range(2):
                ag_wait(k - 1, p, direction)
                ag(k, p, direction).start()
        transpose_bc(k)
        return 0

    mid = max(1, half // 2)
    lax.fori_loop(1, mid, ag_step, 0)

    for n in range(2):
        for c in wx[n]:
            c.wait_recv()
    down_j = mod(x - 1, NX)
    up_j = mod(x + 1, NX)
    far_j = mod(x + 2, NX)
    fw_up = remote(wrow(xw, down_j), wrow(xw, down_j), ws.at[4], wr.at[4], x_up)
    fw_down = remote(wrow(zw, up_j), wrow(zw, up_j), ws.at[5], wr.at[5], x_down)
    fw_up.start()
    fw_down.start()
    sib = []
    for n, (buf, j) in enumerate(((zw, down_j), (zw, up_j), (xw, down_j), (xw, up_j), (zw, far_j), (xw, far_j))):
        sib.append(remote(wrow(buf, j), wrow(buf, j), sibs.at[n], sibr.at[n], sibling))
    for n in range(4):
        sib[n].start()

    lax.fori_loop(mid, half - 1, ag_step, 0)

    k_last = half - 1
    for p in range(2):
        for direction in range(2):
            ag_wait(k_last - 1, p, direction)
            if p == direction:
                ag(k_last, p, direction).start()
    transpose_bc(k_last)

    ow_up = remote(ow_in.at[half_in], wrow(ow, x), ws.at[6], wr.at[6], x_up)
    ow_down = remote(ow_in.at[half_in], wrow(ow, x), ws.at[7], wr.at[7], x_down)
    ow_up.start()
    ow_down.start()

    for c in small:
        c.wait_recv()
    swf[...] = jnp.zeros_like(swf)
    for r in range(nz):
        for j in range(NX):
            swf[j : j + 1, 128 * r : 128 * r + 128] = par[j, r : r + 1, :]
    low = lax.broadcasted_iota(jnp.int32, (8, 128), 1) < 64
    pt[...] = jnp.zeros_like(pt)
    for n in range(2):
        pair = jnp.where(low, par[2 * n, 16:24, :], par[2 * n + 1, 16:24, :])
        pt[0:8, 128 * n : 128 * n + 128] = pair
    pt[0:4, 256:512] = bck_in[...]
    ptt[...] = pt[...].T

    fw_up.wait_recv()
    fw_down.wait_recv()
    sib[4].start()
    sib[5].start()

    ag_wait(k_last, 0, 0)
    ag_wait(k_last, 1, 1)

    tokens = tok[...]
    step_raw = dot(swf[...].astype(BF16), tokens)
    xin[256:512, :] = dot(bct[...], tokens).astype(BF16)
    for c in sib:
        c.wait_recv()
    xin[0:256, :] = dot(xw[...], tokens).astype(BF16)

    pick_r = lax.broadcasted_iota(jnp.int32, (16, BLK), 0)
    pick_c = lax.broadcasted_iota(jnp.int32, (16, BLK), 1)
    pick = jnp.where((pick_c == pick_r + BLK - 3) & (pick_r < 3), 1.0, 0.0).astype(BF16)
    halo_s[...] = dot(pick, xin[...], BOTH).astype(BF16)
    halo = remote(halo_s, halo_r, hsem.at[0], hsem.at[1], next_dev)
    halo.start()

    ow_up.wait_recv()
    ow_down.wait_recv()

    def orow(j, part):
        return rows(ow, 64 * j + hr + 16 * part, 16)

    ofw_up = remote(orow(down_j, 0), orow(down_j, 0), ws.at[8], wr.at[8], x_up)
    ofw_down = remote(orow(up_j, 1), orow(up_j, 1), ws.at[9], wr.at[9], x_down)
    ofw_up.start()
    ofw_down.start()
    osib = []
    for n, j in enumerate((down_j, up_j, far_j)):
        osib.append(remote(wrow(ow, j), wrow(ow, j), sibs.at[6 + n], sibr.at[6 + n], sibling))
    osib[0].start()
    osib[1].start()

    def heads_col(r):
        col = jnp.concatenate([par[j, r : r + 1, :] for j in range(NX)] + [jnp.zeros((4, 128), F32)], axis=0)
        return jnp.concatenate([col, col], axis=1)

    arg = step_raw + heads_col(21)
    u = jnp.exp(-jnp.abs(arg))
    log1p = jnp.where(u < 0.02, u * (1.0 - u * (0.5 - u * (1.0 / 3.0 - u * (0.25 - u * 0.2)))), jnp.log(1.0 + u))
    step = jnp.maximum(arg, 0.0) + log1p
    rate = -jnp.exp(heads_col(22)) * step
    hi = rate.astype(BF16)
    rest = rate - hi.astype(F32)
    mid_part = rest.astype(BF16)
    lo = (rest - mid_part.astype(F32)).astype(BF16)
    ir = lax.broadcasted_iota(jnp.int32, (BLK, BLK), 0)
    ic = lax.broadcasted_iota(jnp.int32, (BLK, BLK), 1)
    tri = jnp.where(ir <= ic, 1.0, 0.0).astype(BF16)
    cum = dot(hi, tri) + dot(mid_part, tri) + dot(lo, tri)
    end = jnp.broadcast_to(cum[:, BLK - 1 : BLK], (8, BLK))
    tail = jnp.exp(end - cum) * step
    grow = jnp.exp(cum)
    tr[...] = jnp.zeros_like(tr)
    tr[0:8, :] = jnp.log(step) - cum
    col_t = tr[...].T

    z_in = dot(zw[...], tokens).astype(BF16).astype(F32)
    zsil[...] = z_in * jax.nn.sigmoid(z_in)

    halo.wait_recv()
    hrow = halo_r[...].astype(F32)
    k0, k1, k2 = pt[0:1, :], pt[1:2, :], pt[2:3, :]
    h0, h1, h2 = hrow[0:1], hrow[1:2], hrow[2:3]
    first = block > 0
    ct[...] = jnp.zeros_like(ct)
    ct[0:1, :] = jnp.where(first, k0 * h0 + k1 * h1 + k2 * h2, 0.0)
    ct[1:2, :] = jnp.where(first, k0 * h1 + k1 * h2, 0.0)
    ct[2:3, :] = jnp.where(first, k0 * h2, 0.0)
    shift = [jnp.where(ic == ir + d, 1.0, 0.0).astype(BF16) for d in range(1, 4)]
    for r in range(4):
        sl = slice(128 * r, 128 * r + 128)
        piece = xin[sl, :]
        taps = ptt[sl, :]
        total = taps[:, 3:4] * piece.astype(F32)
        for d in range(1, 4):
            total = total + taps[:, 3 - d : 4 - d] * dot(piece, shift[d - 1])
        corr = ct[:, sl].T
        total = jnp.concatenate([total[:, :128] + corr, total[:, 128:]], axis=1)
        total = total * jax.nn.sigmoid(total)
        if r < 2:
            xc[sl, :] = total.astype(BF16)
            for n in range(2):
                j = 2 * r + n
                wt[64 * j : 64 * j + 64, :] = (
                    total[64 * n : 64 * n + 64].astype(BF16).astype(F32) * tail[j : j + 1, :]
                ).astype(BF16)
        elif r == 2:
            b_rows = total.T.astype(BF16)
        else:
            c_cols = total.astype(BF16)

    loc = dot(wt[...], b_rows)
    for j in range(NX):
        st1s[j, 0:64, :] = loc[64 * j : 64 * j + 64]
        st1s[j, 64:72, :] = jnp.broadcast_to(end[j : j + 1, 0:128], (8, 128))
    st1r[x] = st1s[x]
    s1 = []
    for d in range(1, NX):
        xp = mod(x + d, NX)
        c = remote(st1s.at[xp], st1r.at[x], s1s.at[d - 1], s1r.at[d - 1], at(s, z, xp))
        c.start()
        s1.append(c)

    ofw_up.wait_recv()
    ofw_down.wait_recv()
    osib[2].start()

    gram = dot(b_rows, c_cols)
    lower = ir[:128, :128] <= ic[:128, :128]

    def intra(j):
        row = cum[j : j + 1, :]
        col = col_t[:, j : j + 1]
        d0 = jnp.where(lower, gram[:128, :128] * jnp.exp(row[:, :128] + col[:128]), 0.0).astype(BF16)
        full = (gram[:128, 128:] * jnp.exp(row[:, 128:] + col[:128])).astype(BF16)
        d1 = jnp.where(lower, gram[128:, 128:] * jnp.exp(row[:, 128:] + col[128:]), 0.0).astype(BF16)
        xj = xc[64 * j : 64 * j + 64, :]
        y0 = dot(xj[:, :128], d0)
        y1 = dot(xj, jnp.concatenate([full, d1], axis=0))
        skip = par[j, 23:24, :]
        y = jnp.concatenate([y0, y1], axis=1) + jnp.concatenate([skip, skip], axis=1) * xj.astype(F32)
        yv[64 * j : 64 * j + 64, :] = y

    intra(0)

    for c in s1:
        c.wait_recv()
    total_state = st1r[0, 0:64, :]
    total_log = st1r[0, 64:72, :]
    for q in range(1, NX):
        log_q = st1r[q, 64:72, :]
        total_state = jnp.exp(log_q[0:1]) * total_state + st1r[q, 0:64, :]
        total_log = total_log + log_q
    st2s[0:64, :] = total_state
    st2s[64:72, :] = total_log

    def s2(t):
        return remote(st2s, st2r.at[s], s2s.at[t - 1], s2r.at[s], (lax.rem(s + t, ns), h))

    for t in range(1, ns):

        @pl.when(s + t < ns)
        def _():
            s2(t).start()

    intra(1)
    intra(2)
    intra(3)

    def take(sp, carry):
        remote(st2s, st2r.at[sp], s2s.at[0], s2r.at[sp], (s, h)).wait_recv()
        factor = jnp.exp(st2r[sp, 64:65, :])
        return factor * carry + st2r[sp, 0:64, :]

    entering = lax.fori_loop(0, s, take, jnp.zeros((64, 128), F32))
    for q in range(NX):
        hs[q] = entering.astype(BF16)
        entering = jnp.exp(st1r[q, 64:65, :]) * entering + st1r[q, 0:64, :]
    held_own = rows(held, 64 * x, 64)
    s3 = []
    for d in range(1, NX):
        xp = mod(x + d, NX)
        c = remote(hs.at[xp], held_own, s3s.at[d - 1], s3r.at[d - 1], at(s, z, xp))
        c.start()
        s3.append(c)
    held[pl.ds(pl.multiple_of(64 * x, 64), 64), :] = hs[x]

    for c in osib:
        c.wait_recv()

    def transpose_ow(k, _):
        at_k = pl.ds(pl.multiple_of(BLK * k, BLK), BLK)
        owt[at_k, :] = ow[:, at_k].T
        return 0

    lax.fori_loop(0, half, transpose_ow, 0)

    for c in s3:
        c.wait_recv()

    square = jnp.zeros((8, BLK), F32)
    for j in range(NX):
        sl = slice(64 * j, 64 * j + 64)
        y = yv[sl, :] + grow[j : j + 1, :] * dot(held[sl, :], c_cols)
        gated = (y * zsil[sl, :]).astype(BF16).astype(F32)
        square = square + jnp.sum((gated * gated).reshape(8, 8, BLK), axis=0)
        sc[sl, :] = (gated * ptt[sl, 4:5]).astype(BF16)
    sqs[...] = jnp.sum(square, axis=0, keepdims=True)

    def partial(dest):
        return dot(owt[pl.ds(pl.multiple_of(128 * dest, 128), 128), :], sc[...])

    send_buf = (rs_rs, rs_ls)
    recv_buf = (rs_rr, rs_lr)

    def rs(k, p, direction):
        part = pl.ds(64 * p, 64)
        to = right if direction == 0 else left
        return remote(
            send_buf[direction].at[k, part],
            recv_buf[direction].at[k, part],
            rss.at[direction, k, p],
            rsr.at[direction, k, p],
            to,
        )

    def rs_dest(k, direction):
        return mod(z + half - k, nz) if direction == 0 else mod(z + nz - half + k, nz)

    for direction in range(2):
        p = direction
        own = partial(rs_dest(0, direction))
        send_buf[direction][0, 64 * p : 64 * p + 64, :] = own[64 * p : 64 * p + 64].astype(BF16)
        rs(0, p, direction).start()

    sq = []
    for d in range(1, nz):
        c = remote(sqs, sqr.at[d - 1], sqss.at[d - 1], sqrs.at[d - 1], at(s, mod(z + d, nz), x))
        c.start()
        sq.append(c)

    own = [partial(rs_dest(1, direction)) for direction in range(2)]
    for direction in range(2):
        p = 1 - direction
        send_buf[direction][1, 64 * p : 64 * p + 64, :] = own[direction][64 * p : 64 * p + 64].astype(BF16)
        rs(1, p, direction).start()
    for direction in range(2):
        p = direction
        rs(0, p, direction).wait_recv()
        got = recv_buf[direction][0, 64 * p : 64 * p + 64, :].astype(F32)
        send_buf[direction][1, 64 * p : 64 * p + 64, :] = (own[direction][64 * p : 64 * p + 64] + got).astype(BF16)
        rs(1, p, direction).start()

    def rs_step(k, _):
        own = [partial(rs_dest(k, direction)) for direction in range(2)]
        for n in range(2):
            for direction in range(2):
                p = (n + 1 - direction) % 2
                rs(k - 1, p, direction).wait_recv()
                part = slice(64 * p, 64 * p + 64)
                got = recv_buf[direction][k - 1, part, :].astype(F32)
                send_buf[direction][k, part, :] = (own[direction][part] + got).astype(BF16)
                rs(k, p, direction).start()
        return 0

    lax.fori_loop(2, half, rs_step, 0)

    own = partial(z)
    total_sq = sqs[...]
    for d in range(1, nz):
        sq[d - 1].wait_recv()
        total_sq = total_sq + sqr[d - 1]
    scale = lax.rsqrt(total_sq / (BLK * nz) + 1e-05)
    for n in range(2):
        for direction in range(2):
            rs(half - 1, (n + 1 - direction) % 2, direction).wait_recv()
    final = own + rs_rr[half - 1].astype(F32) + rs_lr[half - 1].astype(F32)
    res[...] = (final * scale).astype(BF16)

    p4 = []
    for d in range(1, NX):
        xp = mod(x + d, NX)
        c = remote(rows(res, 32 * xp, 32), out_ref.at[:, my_cols], p4s.at[d - 1], p4r.at[d - 1], at(s, z, xp))
        c.start()
        p4.append(c)
    keep = pltpu.make_async_copy(rows(res, 32 * x, 32), out_ref.at[:, my_cols], lsem.at[0])
    keep.start()

    for c in p1 + small + [c for pair in wx for c in pair] + [fw_up, fw_down] + sib:
        c.wait_send()
    for c in [ow_up, ow_down, ofw_up, ofw_down] + osib + [halo] + s1 + s3 + sq:
        c.wait_send()

    def ag_sent(k, _):
        for p in range(2):
            for direction in range(2):
                ag(k, p, direction).wait_send()
        return 0

    lax.fori_loop(0, half - 1, ag_sent, 0)
    for p in range(2):
        ag(half - 1, p, p).wait_send()
        rs(0, p, p).wait_send()

    def rs_sent(k, _):
        for p in range(2):
            for direction in range(2):
                rs(k, p, direction).wait_send()
        return 0

    lax.fori_loop(1, half, rs_sent, 0)
    for t in range(1, ns):

        @pl.when(s + t < ns)
        def _():
            s2(t).wait_send()

    for c in p4:
        c.wait()
    keep.wait()


def solution(mesh):
    ns = mesh.shape["seq"]
    nz = mesh.shape["head"] // NX
    half = nz // 2

    def body(tokens, z_weight, x_weight, bc_weight, step_weight, x_kernel, bc_kernel, step_bias, log_decay, skip_gain, norm_gain, out_weight):
        width = bc_weight.shape[0]
        vmem = pl.BlockSpec(memory_space=pltpu.VMEM)
        hbm = pl.BlockSpec(memory_space=pl.ANY)
        smem = pl.BlockSpec(memory_space=pltpu.SMEM)
        dma = pltpu.SemaphoreType.DMA

        def buf(*shape, dtype=BF16):
            return pltpu.VMEM(shape, dtype)

        out = pl.pallas_call(
            functools.partial(kernel, ns, nz),
            out_shape=jax.ShapeDtypeStruct((32, 4 * BLK), BF16),
            in_specs=[hbm, hbm, hbm, hbm, vmem, vmem, vmem, smem, smem, smem, vmem, hbm],
            out_specs=vmem,
            scratch_shapes=[
                buf(width, BLK),
                buf(256, width),
                buf(256, width),
                buf(width, 256),
                buf(256, width),
                buf(256, width),
                buf(width, 256),
                buf(NX, 24, 128, dtype=F32),
                buf(8, width, dtype=F32),
                buf(128, 512, dtype=F32),
                buf(512, 128, dtype=F32),
                buf(128, 512, dtype=F32),
                buf(512, BLK),
                buf(256, BLK, dtype=F32),
                buf(256, BLK),
                buf(16, 512),
                buf(16, 512),
                buf(128, BLK, dtype=F32),
                buf(16, 128, dtype=F32),
                buf(256, BLK),
                buf(256, BLK, dtype=F32),
                buf(NX, 72, 128, dtype=F32),
                buf(NX, 72, 128, dtype=F32),
                buf(72, 128, dtype=F32),
                buf(ns, 72, 128, dtype=F32),
                buf(NX, 64, 128),
                buf(256, 128),
                buf(1, BLK, dtype=F32),
                buf(nz - 1, 1, BLK, dtype=F32),
                buf(256, BLK),
                buf(half, 128, BLK),
                buf(half, 128, BLK),
                buf(half, 128, BLK),
                buf(half, 128, BLK),
                buf(128, BLK),
                dma((5,)),
                dma((3,)),
                dma((3,)),
                dma((10,)),
                dma((10,)),
                dma((9,)),
                dma((9,)),
                dma((3,)),
                dma((3,)),
                dma((2, half, 2)),
                dma((2, half, 2)),
                dma((2,)),
                dma((3,)),
                dma((3,)),
                dma((ns - 1,)),
                dma((ns,)),
                dma((3,)),
                dma((3,)),
                dma((nz - 1,)),
                dma((nz - 1,)),
                dma((2, half, 2)),
                dma((2, half, 2)),
                dma((3,)),
                dma((3,)),
            ],
            compiler_params=pltpu.CompilerParams(
                collective_id=0, has_side_effects=True, vmem_limit_bytes=40 * 1024 * 1024
            ),
        )(
            tokens.T,
            z_weight.T,
            x_weight.T,
            bc_weight,
            step_weight.T,
            x_kernel,
            bc_kernel,
            step_bias,
            log_decay,
            skip_gain,
            norm_gain.reshape(1, -1),
            out_weight,
        )
        return out.T

    return jax.shard_map(
        body,
        mesh=mesh,
        in_specs=(
            P("seq", "head"),
            P(None, "head"),
            P(None, "head"),
            P(),
            P(None, "head"),
            P(None, "head"),
            P(),
            P("head"),
            P("head"),
            P("head"),
            P("head"),
            P("head", None),
        ),
        out_specs=P("seq", "head"),
        check_vma=False,
    )
```

```python
import functools

import jax
import jax.numpy as jnp
from jax import lax
from jax.experimental import pallas as pl
from jax.experimental.pallas import tpu as pltpu
from jax.sharding import PartitionSpec as P

MESH = pl.DeviceIdType.MESH
F32 = jnp.float32
BF16 = jnp.bfloat16
NX = 4
BLK = 256
DELTAS = (2, -2, 1, -1, 0)
NONE = (((1,), (0,)), ((), ()))
BOTH = (((1,), (1,)), ((), ()))


def dot(a, b, dims=NONE):
    return lax.dot_general(a, b, dims, preferred_element_type=F32)


def kernel(
    ns,
    nz,
    tok_in,
    zw_in,
    xw_in,
    bcw_in,
    sw_in,
    xk_in,
    bck_in,
    bias_in,
    decay_in,
    skip_in,
    gain_in,
    ow_in,
    out_ref,
    tok,
    zw,
    xw,
    bcw,
    bct,
    ow,
    owt,
    par,
    swf,
    pt,
    ptt,
    ct,
    xin,
    zsil,
    xc,
    halo_s,
    halo_r,
    tr,
    bcv,
    wt,
    yv,
    st1s,
    st1r,
    st2s,
    st2r,
    hs,
    held,
    sqs,
    sqr,
    sc,
    sqt,
    sqx,
    rs_s,
    rs_r,
    fin_s,
    fin_r,
    lsem,
    p1s,
    p1r,
    ws,
    wr,
    sibs,
    sibr,
    ps,
    pr,
    ags,
    agr,
    hsem,
    s1s,
    s1r,
    s2s,
    s2r,
    s3s,
    s3r,
    sqss,
    sqrs,
    sqts,
    sqtr,
    rss,
    rsr,
    fins,
    finr,
):
    half = nz // 2
    width = 128 * nz
    s = lax.axis_index("seq")
    h = lax.axis_index("head")
    z = h // NX
    x = lax.rem(h, NX)
    core = lax.rem(s, 2)
    block = s * NX + x
    blocks = ns * NX

    def at(s_to, z_to, x_to):
        return (s_to, z_to * NX + x_to)

    def mod(v, n):
        return lax.rem(v + n, n)

    x_up = at(s, z, mod(x + 1, NX))
    x_down = at(s, z, mod(x - 1, NX))
    sibling = (s + 1 - 2 * core, h)
    after = mod(block + 1, blocks)
    before = mod(block - 1, blocks)
    next_dev = at(after // NX, z, lax.rem(after, NX))
    prev_dev = at(before // NX, z, lax.rem(before, NX))

    def remote(src, dst, send, recv, to):
        return pltpu.make_async_remote_copy(
            src_ref=src, dst_ref=dst, send_sem=send, recv_sem=recv, device_id=to, device_id_type=MESH
        )

    def rows(ref, start, count):
        return ref.at[pl.ds(pl.multiple_of(start, count), count)]

    own_tok = rows(tok, 128 * z + 32 * x, 32)
    my_cols = pl.ds(pl.multiple_of(BLK * x, BLK), BLK)
    local = [
        pltpu.make_async_copy(tok_in.at[:, my_cols], own_tok, lsem.at[0]),
        pltpu.make_async_copy(bcw_in, bcw, lsem.at[1]),
        pltpu.make_async_copy(zw_in, rows(zw, 64 * x, 64), lsem.at[2]),
        pltpu.make_async_copy(xw_in, rows(xw, 64 * x, 64), lsem.at[3]),
        pltpu.make_async_copy(ow_in, rows(ow, 64 * x, 64), lsem.at[4]),
    ]
    for c in local:
        c.start()

    barrier = pltpu.get_barrier_semaphore()

    def greet(to):
        pl.semaphore_signal(barrier, inc=1, device_id=to, device_id_type=MESH)

    for delta in DELTAS:
        for d in range(NX):
            if (delta, d) != (0, 0):
                greet(at(s, mod(z + delta, nz), mod(x + d, NX)))
    for d in range(3, nz - 2):
        greet(at(s, mod(z + d, nz), x))
    for d in range(1, ns):
        greet((mod(s + d, ns), h))
    greet(next_dev)
    greet(prev_dev)

    par[x] = jnp.zeros((24, 128), F32)
    sw = sw_in[...].astype(F32)
    for r in range(nz):
        par[x, r : r + 1, :] = sw[:, 128 * r : 128 * r + 128]
    xk = xk_in[...]
    par[x, 16:20, :] = jnp.concatenate([xk, xk], axis=1)
    gain = gain_in[...].astype(F32)
    par[x, 20:21, :] = jnp.concatenate([gain, gain], axis=1)
    par[x, 21:22, :] = jnp.full((1, 128), bias_in[0], F32)
    par[x, 22:23, :] = jnp.full((1, 128), decay_in[0], F32)
    par[x, 23:24, :] = jnp.full((1, 128), skip_in[0], F32)

    pl.semaphore_wait(barrier, 5 * NX - 1 + (nz - 5) + (ns - 1) + 2)

    def first(i, d):
        xp = mod(x + d, NX)
        cols = pl.ds(pl.multiple_of(BLK * xp, BLK), BLK)
        to = at(s, mod(z + DELTAS[i], nz), xp)
        return remote(tok_in.at[:, cols], own_tok, p1s.at[i, d], p1r.at[i, d], to)

    def first_wait(i, xp):
        d = mod(x - xp, NX)
        ref = rows(tok, 128 * mod(z - DELTAS[i], nz) + 32 * xp, 32)
        remote(ref, ref, p1s.at[i, d], p1r.at[i, d], x_up).wait_recv()

    first_sends = [first(i, d) for i in range(5) for d in range(NX) if (DELTAS[i], d) != (0, 0)]
    for c in first_sends:
        c.start()
    small = []
    for d in range(1, NX):
        c = remote(par.at[x], par.at[x], ps.at[d - 1], pr.at[d - 1], at(s, z, mod(x + d, NX)))
        c.start()
        small.append(c)

    hr = 32 * core

    def wrow(ref, j):
        return rows(ref, 64 * j + hr, 32)

    half_in = pl.ds(pl.multiple_of(hr, 32), 32)
    wx = []
    for n, (src, buf) in enumerate(((zw_in, zw), (xw_in, xw))):
        up = remote(src.at[half_in], wrow(buf, x), ws.at[2 * n], wr.at[2 * n], x_up)
        down = remote(src.at[half_in], wrow(buf, x), ws.at[2 * n + 1], wr.at[2 * n + 1], x_down)
        wx.append((up, down))

    def ag(k, p, direction, even):
        sign = 1 - 2 * direction
        ref = rows(tok, 128 * mod(z - 2 * sign * k, nz) + 64 * p, 64)
        to = at(s, mod(z + sign * (1 + even), nz), x)
        return remote(ref, ref, ags.at[direction, k, p, even], agr.at[direction, k, p, even], to)

    def ag_wait(k, p, direction, even):
        sign = 1 - 2 * direction
        ref = rows(tok, 128 * mod(z - sign * (2 * k + 1 + even), nz) + 64 * p, 64)
        remote(ref, ref, ags.at[direction, k, p, even], agr.at[direction, k, p, even], x_up).wait_recv()

    def ag_has(k, p, direction, even):
        return not even or 2 * k + 2 < half or p == direction

    ag_sends = []

    def ag_step(k):
        for p in range(2):
            for direction in range(2):
                if k == 1:
                    first_wait(direction, 2 * p)
                    first_wait(direction, 2 * p + 1)
                else:
                    ag_wait(k - 1, p, direction, 1)
                for even in (1, 0):
                    if ag_has(k, p, direction, even):
                        c = ag(k, p, direction, even)
                        c.start()
                        ag_sends.append(c)

    def transpose_bc(k, _):
        at_k = pl.ds(pl.multiple_of(BLK * k, BLK), BLK)
        bct[:, at_k] = bcw[at_k, :].T
        return 0

    last = half // 2 - 1
    local[1].wait()
    lax.fori_loop(0, half // 2, transpose_bc, 0)
    ag_step(1)
    wx[1][0].start()
    wx[0][1].start()
    wx[0][0].start()
    wx[1][1].start()
    lax.fori_loop(half // 2, half, transpose_bc, 0)
    for c in small:
        c.wait_recv()
    swf[...] = jnp.zeros_like(swf)
    for r in range(nz):
        for j in range(NX):
            swf[j : j + 1, 128 * r : 128 * r + 128] = par[j, r : r + 1, :]
    low = lax.broadcasted_iota(jnp.int32, (8, 128), 1) < 64
    pt[...] = jnp.zeros_like(pt)
    for n in range(2):
        pair = jnp.where(low, par[2 * n, 16:24, :], par[2 * n + 1, 16:24, :])
        pt[0:8, 128 * n : 128 * n + 128] = pair
    pt[0:4, 256:512] = bck_in[...]
    ptt[...] = pt[...].T
    for k in range(2, last):
        ag_step(k)

    for n in (0, 2, 3, 4):
        local[n].wait()
    for n in range(2):
        for c in wx[n]:
            c.wait_recv()
    down_j = mod(x - 1, NX)
    up_j = mod(x + 1, NX)
    far_j = mod(x + 2, NX)
    fw_up = remote(wrow(xw, down_j), wrow(xw, down_j), ws.at[4], wr.at[4], x_up)
    fw_down = remote(wrow(zw, up_j), wrow(zw, up_j), ws.at[5], wr.at[5], x_down)
    fw_up.start()
    fw_down.start()
    sib = []
    for n, (buf, j) in enumerate(((zw, down_j), (zw, up_j), (xw, down_j), (xw, up_j), (zw, far_j), (xw, far_j))):
        sib.append(remote(wrow(buf, j), wrow(buf, j), sibs.at[n], sibr.at[n], sibling))
    for n in range(4):
        sib[n].start()
    if last > 1:
        ag_step(last)

    ow_up = remote(ow_in.at[half_in], wrow(ow, x), ws.at[6], wr.at[6], x_up)
    ow_down = remote(ow_in.at[half_in], wrow(ow, x), ws.at[7], wr.at[7], x_down)
    ow_up.start()
    ow_down.start()

    fw_up.wait_recv()
    fw_down.wait_recv()
    sib[4].start()
    sib[5].start()

    for i in (2, 3):
        for xp in range(NX):
            first_wait(i, xp)
    for d in range(1, NX):
        first_wait(4, mod(x - d, NX))
    for k in range(1, last + 1):
        for p in range(2):
            for direction in range(2):
                ag_wait(k, p, direction, 0)
                if k == last and ag_has(k, p, direction, 1):
                    ag_wait(k, p, direction, 1)

    tokens = tok[...]
    step_raw = dot(swf[...].astype(BF16), tokens)
    xin[256:512, :] = dot(bct[...], tokens).astype(BF16)
    for c in sib:
        c.wait_recv()
    xin[0:256, :] = dot(xw[...], tokens).astype(BF16)

    pick_r = lax.broadcasted_iota(jnp.int32, (16, BLK), 0)
    pick_c = lax.broadcasted_iota(jnp.int32, (16, BLK), 1)
    pick = jnp.where((pick_c == pick_r + BLK - 3) & (pick_r < 3), 1.0, 0.0).astype(BF16)
    halo_s[...] = dot(pick, xin[...], BOTH).astype(BF16)
    halo = remote(halo_s, halo_r, hsem.at[0], hsem.at[1], next_dev)
    halo.start()

    ow_up.wait_recv()
    ow_down.wait_recv()

    def orow(j, part):
        return rows(ow, 64 * j + hr + 16 * part, 16)

    ofw_up = remote(orow(down_j, 0), orow(down_j, 0), ws.at[8], wr.at[8], x_up)
    ofw_down = remote(orow(up_j, 1), orow(up_j, 1), ws.at[9], wr.at[9], x_down)
    ofw_up.start()
    ofw_down.start()
    osib = []
    for n, j in enumerate((down_j, up_j, far_j)):
        osib.append(remote(wrow(ow, j), wrow(ow, j), sibs.at[6 + n], sibr.at[6 + n], sibling))
    osib[0].start()
    osib[1].start()

    def heads_col(r):
        col = jnp.concatenate([par[j, r : r + 1, :] for j in range(NX)] + [jnp.zeros((4, 128), F32)], axis=0)
        return jnp.concatenate([col, col], axis=1)

    arg = step_raw + heads_col(21)
    u = jnp.exp(-jnp.abs(arg))
    log1p = jnp.where(u < 0.02, u * (1.0 - u * (0.5 - u * (1.0 / 3.0 - u * (0.25 - u * 0.2)))), jnp.log(1.0 + u))
    step = jnp.maximum(arg, 0.0) + log1p
    rate = -jnp.exp(heads_col(22)) * step
    hi = rate.astype(BF16)
    rest = rate - hi.astype(F32)
    mid_part = rest.astype(BF16)
    lo = (rest - mid_part.astype(F32)).astype(BF16)
    ir = lax.broadcasted_iota(jnp.int32, (BLK, BLK), 0)
    ic = lax.broadcasted_iota(jnp.int32, (BLK, BLK), 1)
    tri = jnp.where(ir <= ic, 1.0, 0.0).astype(BF16)
    cum = dot(hi, tri) + dot(mid_part, tri) + dot(lo, tri)
    end = jnp.broadcast_to(cum[:, BLK - 1 : BLK], (8, BLK))
    tail = jnp.exp(end - cum) * step
    grow = jnp.exp(cum)
    tr[...] = jnp.zeros_like(tr)
    tr[0:8, :] = jnp.log(step) - cum
    col_t = tr[...].T

    z_in = dot(zw[...], tokens).astype(BF16).astype(F32)
    zsil[...] = z_in * jax.nn.sigmoid(z_in)

    halo.wait_recv()
    hrow = halo_r[...].astype(F32)
    k0, k1, k2 = pt[0:1, :], pt[1:2, :], pt[2:3, :]
    h0, h1, h2 = hrow[0:1], hrow[1:2], hrow[2:3]
    first = block > 0
    ct[...] = jnp.zeros_like(ct)
    ct[0:1, :] = jnp.where(first, k0 * h0 + k1 * h1 + k2 * h2, 0.0)
    ct[1:2, :] = jnp.where(first, k0 * h1 + k1 * h2, 0.0)
    ct[2:3, :] = jnp.where(first, k0 * h2, 0.0)
    shift = [jnp.where(ic == ir + d, 1.0, 0.0).astype(BF16) for d in range(1, 4)]
    for r in range(4):
        sl = slice(128 * r, 128 * r + 128)
        piece = xin[sl, :]
        taps = ptt[sl, :]
        total = taps[:, 3:4] * piece.astype(F32)
        for d in range(1, 4):
            total = total + taps[:, 3 - d : 4 - d] * dot(piece, shift[d - 1])
        corr = ct[:, sl].T
        total = jnp.concatenate([total[:, :128] + corr, total[:, 128:]], axis=1)
        total = total * jax.nn.sigmoid(total)
        if r < 2:
            xc[sl, :] = total.astype(BF16)
            for n in range(2):
                j = 2 * r + n
                wt[64 * j : 64 * j + 64, :] = (
                    total[64 * n : 64 * n + 64].astype(BF16).astype(F32) * tail[j : j + 1, :]
                ).astype(BF16)
        elif r == 2:
            b_rows = total.T.astype(BF16)
        else:
            c_cols = total.astype(BF16)

    loc = dot(wt[...], b_rows)
    for j in range(NX):
        st1s[j, 0:64, :] = loc[64 * j : 64 * j + 64]
        st1s[j, 64:72, :] = jnp.broadcast_to(end[j : j + 1, 0:128], (8, 128))
    st1r[x] = st1s[x]
    s1 = []
    for d in range(1, NX):
        xp = mod(x + d, NX)
        c = remote(st1s.at[xp], st1r.at[x], s1s.at[d - 1], s1r.at[d - 1], at(s, z, xp))
        c.start()
        s1.append(c)

    ofw_up.wait_recv()
    ofw_down.wait_recv()
    osib[2].start()

    gram = dot(b_rows, c_cols)
    lower = ir[:128, :128] <= ic[:128, :128]

    def intra(j):
        row = cum[j : j + 1, :]
        col = col_t[:, j : j + 1]
        d0 = jnp.where(lower, gram[:128, :128] * jnp.exp(row[:, :128] + col[:128]), 0.0).astype(BF16)
        full = (gram[:128, 128:] * jnp.exp(row[:, 128:] + col[:128])).astype(BF16)
        d1 = jnp.where(lower, gram[128:, 128:] * jnp.exp(row[:, 128:] + col[128:]), 0.0).astype(BF16)
        xj = xc[64 * j : 64 * j + 64, :]
        y0 = dot(xj[:, :128], d0)
        y1 = dot(xj, jnp.concatenate([full, d1], axis=0))
        skip = par[j, 23:24, :]
        y = jnp.concatenate([y0, y1], axis=1) + jnp.concatenate([skip, skip], axis=1) * xj.astype(F32)
        yv[64 * j : 64 * j + 64, :] = y

    intra(0)

    for c in s1:
        c.wait_recv()
    total_state = st1r[0, 0:64, :]
    total_log = st1r[0, 64:72, :]
    for q in range(1, NX):
        log_q = st1r[q, 64:72, :]
        total_state = jnp.exp(log_q[0:1]) * total_state + st1r[q, 0:64, :]
        total_log = total_log + log_q
    st2s[0:64, :] = total_state
    st2s[64:72, :] = total_log

    def s2(t):
        return remote(st2s, st2r.at[s], s2s.at[t - 1], s2r.at[s], (lax.rem(s + t, ns), h))

    for t in range(1, ns):

        @pl.when(s + t < ns)
        def _():
            s2(t).start()

    intra(1)
    intra(2)
    intra(3)

    def take(sp, carry):
        remote(st2s, st2r.at[sp], s2s.at[0], s2r.at[sp], (s, h)).wait_recv()
        factor = jnp.exp(st2r[sp, 64:65, :])
        return factor * carry + st2r[sp, 0:64, :]

    entering = lax.fori_loop(0, s, take, jnp.zeros((64, 128), F32))
    for q in range(NX):
        hs[q] = entering.astype(BF16)
        entering = jnp.exp(st1r[q, 64:65, :]) * entering + st1r[q, 0:64, :]
    held_own = rows(held, 64 * x, 64)
    s3 = []
    for d in range(1, NX):
        xp = mod(x + d, NX)
        c = remote(hs.at[xp], held_own, s3s.at[d - 1], s3r.at[d - 1], at(s, z, xp))
        c.start()
        s3.append(c)
    held[pl.ds(pl.multiple_of(64 * x, 64), 64), :] = hs[x]

    for c in osib:
        c.wait_recv()

    def transpose_ow(k, _):
        at_k = pl.ds(pl.multiple_of(BLK * k, BLK), BLK)
        owt[at_k, :] = ow[:, at_k].T
        return 0

    lax.fori_loop(0, half, transpose_ow, 0)

    for c in s3:
        c.wait_recv()

    square = jnp.zeros((8, BLK), F32)
    for j in range(NX):
        sl = slice(64 * j, 64 * j + 64)
        y = yv[sl, :] + grow[j : j + 1, :] * dot(held[sl, :], c_cols)
        gated = (y * zsil[sl, :]).astype(BF16).astype(F32)
        square = square + jnp.sum((gated * gated).reshape(8, 8, BLK), axis=0)
        sc[sl, :] = (gated * ptt[sl, 4:5]).astype(BF16)
    sqs[...] = jnp.sum(square, axis=0, keepdims=True)

    def partial(dest):
        return dot(owt[pl.ds(pl.multiple_of(128 * dest, 128), 128), :], sc[...])

    def rs(m, p, direction, to):
        part = pl.ds(64 * p, 64)
        return remote(
            rs_s.at[direction, m, part], rs_r.at[direction, m, part], rss.at[direction, m, p], rsr.at[direction, m, p], to
        )

    rs_sends = []

    def rs_start(m, p, direction):
        step = 1 if m % 2 else 2
        c = rs(m, p, direction, at(s, mod(z + (1 - 2 * direction) * step, nz), x))
        c.start()
        rs_sends.append(c)

    def fin_start(i):
        for d in range(NX):
            if (DELTAS[i], d) != (0, 0):
                xp = mod(x + d, NX)
                src = fin_s.at[i, pl.ds(pl.multiple_of(32 * xp, 32), 32)]
                c = remote(src, fin_r.at[i, d], fins.at[i, d], finr.at[i, d], at(s, mod(z + DELTAS[i], nz), xp))
                c.start()
                rs_sends.append(c)

    def own(m, direction):
        return partial(mod(z + (1 - 2 * direction) * m, nz))

    def leaf(m):
        for direction in range(2):
            value = own(m, direction).astype(BF16)
            if m == 1:
                fin_s[2 + direction] = value
                fin_start(2 + direction)
                continue
            rs_s[direction, m] = value
            for p in range(2):
                if m < half or p == direction:
                    rs_start(m, p, direction)

    leaf(half)
    leaf(half - 1)
    sq = []
    for d in range(1, nz):
        c = remote(sqs, sqr.at[d - 1], sqss.at[d - 1], sqrs.at[d - 1], at(s, mod(z + d, nz), x))
        c.start()
        sq.append(c)
    leaf(half - 3)

    mine = partial(z)
    fin_s[4] = mine.astype(BF16)
    sqt_sends = []
    for m in range(half - 2, 0, -2):
        values = [own(m, direction) for direction in range(2)]
        for p in range(2):
            part = slice(64 * p, 64 * p + 64)
            for direction in range(2):
                rs(m + 1, p, direction, x_up).wait_recv()
                value = values[direction][part] + rs_r[direction, m + 1, part, :].astype(F32)
                if m + 2 < half or p == direction:
                    rs(m + 2, p, direction, x_up).wait_recv()
                    value = value + rs_r[direction, m + 2, part, :].astype(F32)
                if m > 2:
                    rs_s[direction, m, part, :] = value.astype(BF16)
                    rs_start(m, p, direction)
                else:
                    fin_s[direction, part, :] = value.astype(BF16)
        if m == 2:
            fin_start(0)
            fin_start(1)
        if m > 3:
            leaf(m - 3)
        if m == half - 2:
            fin_start(4)
            total_sq = sqs[...]
            for d in range(1, nz):
                sq[d - 1].wait_recv()
                total_sq = total_sq + sqr[d - 1]
            sqt[...] = total_sq
            for d in range(1, NX):
                c = remote(sqt, sqx.at[d - 1], sqts.at[d - 1], sqtr.at[d - 1], at(s, z, mod(x + d, NX)))
                c.start()
                sqt_sends.append(c)

    for d in range(NX):
        if d > 0:
            sqt_sends[d - 1].wait_recv()
            squares = sqx[d - 1]
        else:
            squares = sqt[...]
        scale = lax.rsqrt(squares / (BLK * nz) + 1e-05)
        if d == 0:
            total = fin_s[4, pl.ds(pl.multiple_of(32 * x, 32), 32), :].astype(F32)
        for i in (4, 2, 3, 0, 1):
            if (DELTAS[i], d) != (0, 0):
                ref = fin_r.at[i, d]
                remote(ref, ref, fins.at[i, d], finr.at[i, d], x_up).wait_recv()
                got = fin_r[i, d].astype(F32)
                total = got if i == 4 else total + got
        from_x = mod(x - d, NX)
        out_ref[:, pl.ds(pl.multiple_of(BLK * from_x, BLK), BLK)] = (total * scale).astype(BF16)

    for c in first_sends + small + [c for pair in wx for c in pair] + [fw_up, fw_down] + sib + ag_sends:
        c.wait_send()
    for c in [ow_up, ow_down, ofw_up, ofw_down] + osib + [halo] + s1 + s3 + sq + sqt_sends + rs_sends:
        c.wait_send()
    for t in range(1, ns):

        @pl.when(s + t < ns)
        def _():
            s2(t).wait_send()


def solution(mesh):
    ns = mesh.shape["seq"]
    nz = mesh.shape["head"] // NX
    half = nz // 2

    def body(tokens, z_weight, x_weight, bc_weight, step_weight, x_kernel, bc_kernel, step_bias, log_decay, skip_gain, norm_gain, out_weight):
        width = bc_weight.shape[0]
        vmem = pl.BlockSpec(memory_space=pltpu.VMEM)
        hbm = pl.BlockSpec(memory_space=pl.ANY)
        smem = pl.BlockSpec(memory_space=pltpu.SMEM)
        dma = pltpu.SemaphoreType.DMA

        def buf(*shape, dtype=BF16):
            return pltpu.VMEM(shape, dtype)

        out = pl.pallas_call(
            functools.partial(kernel, ns, nz),
            out_shape=jax.ShapeDtypeStruct((32, 4 * BLK), BF16),
            in_specs=[hbm, hbm, hbm, hbm, vmem, vmem, vmem, smem, smem, smem, vmem, hbm],
            out_specs=vmem,
            scratch_shapes=[
                buf(width, BLK),
                buf(256, width),
                buf(256, width),
                buf(width, 256),
                buf(256, width),
                buf(256, width),
                buf(width, 256),
                buf(NX, 24, 128, dtype=F32),
                buf(8, width, dtype=F32),
                buf(128, 512, dtype=F32),
                buf(512, 128, dtype=F32),
                buf(128, 512, dtype=F32),
                buf(512, BLK),
                buf(256, BLK, dtype=F32),
                buf(256, BLK),
                buf(16, 512),
                buf(16, 512),
                buf(128, BLK, dtype=F32),
                buf(16, 128, dtype=F32),
                buf(256, BLK),
                buf(256, BLK, dtype=F32),
                buf(NX, 72, 128, dtype=F32),
                buf(NX, 72, 128, dtype=F32),
                buf(72, 128, dtype=F32),
                buf(ns, 72, 128, dtype=F32),
                buf(NX, 64, 128),
                buf(256, 128),
                buf(1, BLK, dtype=F32),
                buf(nz - 1, 1, BLK, dtype=F32),
                buf(256, BLK),
                buf(1, BLK, dtype=F32),
                buf(NX - 1, 1, BLK, dtype=F32),
                buf(2, half + 1, 128, BLK),
                buf(2, half + 1, 128, BLK),
                buf(5, 128, BLK),
                buf(5, NX, 32, BLK),
                dma((5,)),
                dma((5, NX)),
                dma((5, NX)),
                dma((10,)),
                dma((10,)),
                dma((9,)),
                dma((9,)),
                dma((3,)),
                dma((3,)),
                dma((2, half // 2, 2, 2)),
                dma((2, half // 2, 2, 2)),
                dma((2,)),
                dma((3,)),
                dma((3,)),
                dma((ns - 1,)),
                dma((ns,)),
                dma((3,)),
                dma((3,)),
                dma((nz - 1,)),
                dma((nz - 1,)),
                dma((3,)),
                dma((3,)),
                dma((2, half + 1, 2)),
                dma((2, half + 1, 2)),
                dma((5, NX)),
                dma((5, NX)),
            ],
            compiler_params=pltpu.CompilerParams(
                collective_id=0, has_side_effects=True, vmem_limit_bytes=60 * 1024 * 1024
            ),
        )(
            tokens.T,
            z_weight.T,
            x_weight.T,
            bc_weight,
            step_weight.T,
            x_kernel,
            bc_kernel,
            step_bias,
            log_decay,
            skip_gain,
            norm_gain.reshape(1, -1),
            out_weight,
        )
        return out.T

    return jax.shard_map(
        body,
        mesh=mesh,
        in_specs=(
            P("seq", "head"),
            P(None, "head"),
            P(None, "head"),
            P(),
            P(None, "head"),
            P(None, "head"),
            P(),
            P("head"),
            P("head"),
            P("head"),
            P("head"),
            P("head", None),
        ),
        out_specs=P("seq", "head"),
        check_vma=False,
    )
```

```python
import functools

import jax
import jax.numpy as jnp
from jax import lax
from jax.experimental import pallas as pl
from jax.experimental.pallas import tpu as pltpu
from jax.sharding import PartitionSpec as P

MESH = pl.DeviceIdType.MESH
F32 = jnp.float32
BF16 = jnp.bfloat16
NX = 4
BLK = 256
DELTAS = (2, -2, 1, -1, 0)
NONE = (((1,), (0,)), ((), ()))
BOTH = (((1,), (1,)), ((), ()))


def dot(a, b, dims=NONE):
    return lax.dot_general(a, b, dims, preferred_element_type=F32)


def kernel(
    ns,
    nz,
    tok_in,
    zw_in,
    xw_in,
    bcw_in,
    sw_in,
    xk_in,
    bck_in,
    bias_in,
    decay_in,
    skip_in,
    gain_in,
    ow_in,
    out_ref,
    tok,
    zw,
    xw,
    bcw,
    bct,
    ow,
    owt,
    par,
    swf,
    pt,
    ptt,
    ct,
    xin,
    zsil,
    xc,
    halo_s,
    halo_r,
    tr,
    bcv,
    wt,
    yv,
    st1s,
    st1r,
    st2s,
    st2r,
    hs,
    held,
    sqs,
    sqr,
    sc,
    sqt,
    sqx,
    rs_s,
    rs_r,
    fin_s,
    fin_r,
    lsem,
    snd,
    p1r,
    p1x,
    wr,
    sibr,
    pr,
    agr,
    ago,
    hsem,
    s1r,
    s2r,
    s3r,
    sqrs,
    sqtr,
    rsr,
    rso,
    finr,
):
    half = nz // 2
    width = 128 * nz
    s = lax.axis_index("seq")
    h = lax.axis_index("head")
    z = h // NX
    x = lax.rem(h, NX)
    core = lax.rem(s, 2)
    block = s * NX + x
    blocks = ns * NX

    def at(s_to, z_to, x_to):
        return (s_to, z_to * NX + x_to)

    def mod(v, n):
        return lax.rem(v + n, n)

    x_up = at(s, z, mod(x + 1, NX))
    x_down = at(s, z, mod(x - 1, NX))
    sibling = (s + 1 - 2 * core, h)
    after = mod(block + 1, blocks)
    before = mod(block - 1, blocks)
    next_dev = at(after // NX, z, lax.rem(after, NX))
    prev_dev = at(before // NX, z, lax.rem(before, NX))

    def remote(src, dst, recv, to, group=0):
        return pltpu.make_async_remote_copy(
            src_ref=src, dst_ref=dst, send_sem=snd.at[group], recv_sem=recv, device_id=to, device_id_type=MESH
        )

    def wait_in(ref, sem):
        remote(ref, ref, sem, sibling).wait_recv()

    def wait_out(ref, group):
        remote(ref, ref, hsem.at[0], sibling, group).wait_send()

    def rows(ref, start, count):
        return ref.at[pl.ds(pl.multiple_of(start, count), count)]

    own_tok = rows(tok, 128 * z + 32 * x, 32)
    my_cols = pl.ds(pl.multiple_of(BLK * x, BLK), BLK)
    local = [
        pltpu.make_async_copy(tok_in.at[:, my_cols], own_tok, lsem.at[0]),
        pltpu.make_async_copy(bcw_in, bcw, lsem.at[1]),
        pltpu.make_async_copy(zw_in, rows(zw, 64 * x, 64), lsem.at[2]),
        pltpu.make_async_copy(xw_in, rows(xw, 64 * x, 64), lsem.at[2]),
        pltpu.make_async_copy(ow_in, rows(ow, 64 * x, 64), lsem.at[2]),
    ]
    for c in local:
        c.start()

    barrier = pltpu.get_barrier_semaphore()

    def greet(to):
        pl.semaphore_signal(barrier, inc=1, device_id=to, device_id_type=MESH)

    for delta in DELTAS:
        for d in range(NX):
            if (delta, d) != (0, 0):
                greet(at(s, mod(z + delta, nz), mod(x + d, NX)))
    for d in range(3, nz - 2):
        greet(at(s, mod(z + d, nz), x))
    for d in range(1, ns):
        greet((mod(s + d, ns), h))
    greet(next_dev)
    greet(prev_dev)

    par[x] = jnp.zeros((24, 128), F32)
    sw = sw_in[...].astype(F32)
    for r in range(nz):
        par[x, r : r + 1, :] = sw[:, 128 * r : 128 * r + 128]
    xk = xk_in[...]
    par[x, 16:20, :] = jnp.concatenate([xk, xk], axis=1)
    gain = gain_in[...].astype(F32)
    par[x, 20:21, :] = jnp.concatenate([gain, gain], axis=1)
    par[x, 21:22, :] = jnp.full((1, 128), bias_in[0], F32)
    par[x, 22:23, :] = jnp.full((1, 128), decay_in[0], F32)
    par[x, 23:24, :] = jnp.full((1, 128), skip_in[0], F32)

    pl.semaphore_wait(barrier, 5 * NX - 1 + (nz - 5) + (ns - 1) + 2)

    def first(i, d):
        xp = mod(x + d, NX)
        cols = pl.ds(pl.multiple_of(BLK * xp, BLK), BLK)
        to = at(s, mod(z + DELTAS[i], nz), xp)
        return remote(tok_in.at[:, cols], own_tok, p1r.at[i, d] if i < 2 else p1x.at[0], to)

    def first_wait(i, xp):
        d = mod(x - xp, NX)
        ref = rows(tok, 128 * mod(z - DELTAS[i], nz) + 32 * xp, 32)
        remote(ref, ref, p1r.at[i, d] if i < 2 else p1x.at[0], x_up).wait_recv()

    first_sends = [first(i, d) for i in range(5) for d in range(NX) if (DELTAS[i], d) != (0, 0)]
    for c in first_sends:
        c.start()
    small = []
    for d in range(1, NX):
        c = remote(par.at[x], par.at[x], pr.at[0], at(s, z, mod(x + d, NX)), 5)
        c.start()
        small.append(c)

    hr = 32 * core

    def wrow(ref, j):
        return rows(ref, 64 * j + hr, 32)

    half_in = pl.ds(pl.multiple_of(hr, 32), 32)
    wx = []
    for n, (src, buf) in enumerate(((zw_in, zw), (xw_in, xw))):
        up = remote(src.at[half_in], wrow(buf, x), wr.at[0], x_up, 2)
        down = remote(src.at[half_in], wrow(buf, x), wr.at[0], x_down, 2)
        wx.append((up, down))
    wx[1][0].start()
    wx[0][1].start()
    wx[0][0].start()
    wx[1][1].start()

    last = half // 2 - 1

    def ag_rows(k, p, even):
        return (0, 128) if not even and k < last else (32 * p, 32)

    def ag_sem(k, p, direction, even):
        return agr.at[direction, k - 1, p] if even else ago.at[int(k == last)]

    def ag(k, p, direction, even):
        sign = 1 - 2 * direction
        start, count = ag_rows(k, p, even)
        ref = rows(tok, 128 * mod(z - 2 * sign * k, nz) + start, count)
        to = at(s, mod(z + sign * (1 + even), nz), x)
        return remote(ref, ref, ag_sem(k, p, direction, even), to)

    def ag_wait(k, p, direction, even):
        sign = 1 - 2 * direction
        start, count = ag_rows(k, p, even)
        ref = rows(tok, 128 * mod(z - sign * (2 * k + 1 + even), nz) + start, count)
        remote(ref, ref, ag_sem(k, p, direction, even), x_up).wait_recv()

    def ag_has(k, p, direction, even):
        if even:
            return k < last or p // 2 == direction
        return k == last or p == 0

    ag_pieces = []

    def ag_step(k):
        for p in range(NX):
            for direction in range(2):
                if k == 1:
                    first_wait(direction, p)
                else:
                    ag_wait(k - 1, p, direction, 1)
                for even in (1, 0):
                    if ag_has(k, p, direction, even) and (even or k == last):
                        c = ag(k, p, direction, even)
                        c.start()
                        ag_pieces.append(1)
        if k < last:
            for direction in range(2):
                c = ag(k, 0, direction, 0)
                c.start()
                ag_pieces.append(4)

    def transpose_bc(k, _):
        at_k = pl.ds(pl.multiple_of(BLK * k, BLK), BLK)
        bct[:, at_k] = bcw[at_k, :].T
        return 0

    local[1].wait()
    lax.fori_loop(0, half // 2, transpose_bc, 0)
    ag_step(1)
    lax.fori_loop(half // 2, half, transpose_bc, 0)
    wait_in(par.at[pl.ds(0, NX - 1)], pr.at[0])
    swf[...] = jnp.zeros_like(swf)
    for r in range(nz):
        for j in range(NX):
            swf[j : j + 1, 128 * r : 128 * r + 128] = par[j, r : r + 1, :]
    low = lax.broadcasted_iota(jnp.int32, (8, 128), 1) < 64
    pt[...] = jnp.zeros_like(pt)
    for n in range(2):
        pair = jnp.where(low, par[2 * n, 16:24, :], par[2 * n + 1, 16:24, :])
        pt[0:8, 128 * n : 128 * n + 128] = pair
    pt[0:4, 256:512] = bck_in[...]
    ptt[...] = pt[...].T
    for k in range(2, last):
        ag_step(k)

    local[0].wait()
    loaded = zw.at[pl.ds(0, 192)]
    pltpu.make_async_copy(loaded, loaded, lsem.at[2]).wait()
    wait_in(zw.at[pl.ds(0, 128)], wr.at[0])
    down_j = mod(x - 1, NX)
    up_j = mod(x + 1, NX)
    far_j = mod(x + 2, NX)
    fw_up = remote(wrow(xw, down_j), wrow(xw, down_j), wr.at[1], x_up, 2)
    fw_down = remote(wrow(zw, up_j), wrow(zw, up_j), wr.at[1], x_down, 2)
    fw_up.start()
    fw_down.start()
    sib = []
    for n, (buf, j) in enumerate(((zw, down_j), (zw, up_j), (xw, down_j), (xw, up_j), (zw, far_j), (xw, far_j))):
        sib.append(remote(wrow(buf, j), wrow(buf, j), sibr.at[0], sibling, 3))
    for n in range(4):
        sib[n].start()
    if last > 1:
        ag_step(last)

    ow_up = remote(ow_in.at[half_in], wrow(ow, x), wr.at[2], x_up, 4)
    ow_down = remote(ow_in.at[half_in], wrow(ow, x), wr.at[2], x_down, 4)
    ow_up.start()
    ow_down.start()

    wait_in(zw.at[pl.ds(0, 64)], wr.at[1])
    sib[4].start()
    sib[5].start()

    wait_in(tok.at[pl.ds(0, 32 * (3 * NX - 1))], p1x.at[0])
    if last > 1:
        wait_in(tok.at[pl.ds(0, 256 * (last - 1))], ago.at[0])
    wait_in(tok.at[pl.ds(0, 256)], ago.at[1])
    for p in range(NX):
        for direction in range(2):
            if ag_has(last, p, direction, 1):
                ag_wait(last, p, direction, 1)

    tokens = tok[...]
    step_raw = dot(swf[...].astype(BF16), tokens)
    xin[256:512, :] = dot(bct[...], tokens).astype(BF16)
    wait_in(zw.at[pl.ds(0, 192)], sibr.at[0])
    xin[0:256, :] = dot(xw[...], tokens).astype(BF16)

    pick_r = lax.broadcasted_iota(jnp.int32, (16, BLK), 0)
    pick_c = lax.broadcasted_iota(jnp.int32, (16, BLK), 1)
    pick = jnp.where((pick_c == pick_r + BLK - 3) & (pick_r < 3), 1.0, 0.0).astype(BF16)
    halo_s[...] = dot(pick, xin[...], BOTH).astype(BF16)
    halo = remote(halo_s, halo_r, hsem.at[0], next_dev, 6)
    halo.start()

    wait_in(ow.at[pl.ds(0, 64)], wr.at[2])

    def orow(j, part):
        return rows(ow, 64 * j + hr + 16 * part, 16)

    ofw_up = remote(orow(down_j, 0), orow(down_j, 0), wr.at[3], x_up, 4)
    ofw_down = remote(orow(up_j, 1), orow(up_j, 1), wr.at[3], x_down, 4)
    ofw_up.start()
    ofw_down.start()
    osib = []
    for n, j in enumerate((down_j, up_j, far_j)):
        osib.append(remote(wrow(ow, j), wrow(ow, j), sibr.at[1], sibling, 4))
    osib[0].start()
    osib[1].start()

    def heads_col(r):
        col = jnp.concatenate([par[j, r : r + 1, :] for j in range(NX)] + [jnp.zeros((4, 128), F32)], axis=0)
        return jnp.concatenate([col, col], axis=1)

    arg = step_raw + heads_col(21)
    u = jnp.exp(-jnp.abs(arg))
    log1p = jnp.where(u < 0.02, u * (1.0 - u * (0.5 - u * (1.0 / 3.0 - u * (0.25 - u * 0.2)))), jnp.log(1.0 + u))
    step = jnp.maximum(arg, 0.0) + log1p
    rate = -jnp.exp(heads_col(22)) * step
    hi = rate.astype(BF16)
    rest = rate - hi.astype(F32)
    mid_part = rest.astype(BF16)
    lo = (rest - mid_part.astype(F32)).astype(BF16)
    ir = lax.broadcasted_iota(jnp.int32, (BLK, BLK), 0)
    ic = lax.broadcasted_iota(jnp.int32, (BLK, BLK), 1)
    tri = jnp.where(ir <= ic, 1.0, 0.0).astype(BF16)
    cum = dot(hi, tri) + dot(mid_part, tri) + dot(lo, tri)
    end = jnp.broadcast_to(cum[:, BLK - 1 : BLK], (8, BLK))
    tail = jnp.exp(end - cum) * step
    grow = jnp.exp(cum)
    tr[...] = jnp.zeros_like(tr)
    tr[0:8, :] = jnp.log(step) - cum
    col_t = tr[...].T

    z_in = dot(zw[...], tokens).astype(BF16).astype(F32)
    zsil[...] = z_in * jax.nn.sigmoid(z_in)

    halo.wait_recv()
    hrow = halo_r[...].astype(F32)
    k0, k1, k2 = pt[0:1, :], pt[1:2, :], pt[2:3, :]
    h0, h1, h2 = hrow[0:1], hrow[1:2], hrow[2:3]
    first = block > 0
    ct[...] = jnp.zeros_like(ct)
    ct[0:1, :] = jnp.where(first, k0 * h0 + k1 * h1 + k2 * h2, 0.0)
    ct[1:2, :] = jnp.where(first, k0 * h1 + k1 * h2, 0.0)
    ct[2:3, :] = jnp.where(first, k0 * h2, 0.0)
    shift = [jnp.where(ic == ir + d, 1.0, 0.0).astype(BF16) for d in range(1, 4)]
    for r in range(4):
        sl = slice(128 * r, 128 * r + 128)
        piece = xin[sl, :]
        taps = ptt[sl, :]
        total = taps[:, 3:4] * piece.astype(F32)
        for d in range(1, 4):
            total = total + taps[:, 3 - d : 4 - d] * dot(piece, shift[d - 1])
        corr = ct[:, sl].T
        total = jnp.concatenate([total[:, :128] + corr, total[:, 128:]], axis=1)
        total = total * jax.nn.sigmoid(total)
        if r < 2:
            xc[sl, :] = total.astype(BF16)
            for n in range(2):
                j = 2 * r + n
                wt[64 * j : 64 * j + 64, :] = (
                    total[64 * n : 64 * n + 64].astype(BF16).astype(F32) * tail[j : j + 1, :]
                ).astype(BF16)
        elif r == 2:
            b_rows = total.T.astype(BF16)
        else:
            c_cols = total.astype(BF16)

    loc = dot(wt[...], b_rows)
    for j in range(NX):
        st1s[j, 0:64, :] = loc[64 * j : 64 * j + 64]
        st1s[j, 64:72, :] = jnp.broadcast_to(end[j : j + 1, 0:128], (8, 128))
    st1r[x] = st1s[x]
    s1 = []
    for d in range(1, NX):
        xp = mod(x + d, NX)
        c = remote(st1s.at[xp], st1r.at[x], s1r.at[0], at(s, z, xp), 7)
        c.start()
        s1.append(c)

    wait_in(ow.at[pl.ds(0, 32)], wr.at[3])
    osib[2].start()

    gram = dot(b_rows, c_cols)
    lower = ir[:128, :128] <= ic[:128, :128]

    def intra(j):
        row = cum[j : j + 1, :]
        col = col_t[:, j : j + 1]
        d0 = jnp.where(lower, gram[:128, :128] * jnp.exp(row[:, :128] + col[:128]), 0.0).astype(BF16)
        full = (gram[:128, 128:] * jnp.exp(row[:, 128:] + col[:128])).astype(BF16)
        d1 = jnp.where(lower, gram[128:, 128:] * jnp.exp(row[:, 128:] + col[128:]), 0.0).astype(BF16)
        xj = xc[64 * j : 64 * j + 64, :]
        y0 = dot(xj[:, :128], d0)
        y1 = dot(xj, jnp.concatenate([full, d1], axis=0))
        skip = par[j, 23:24, :]
        y = jnp.concatenate([y0, y1], axis=1) + jnp.concatenate([skip, skip], axis=1) * xj.astype(F32)
        yv[64 * j : 64 * j + 64, :] = y

    intra(0)

    wait_in(st1r.at[pl.ds(0, NX - 1)], s1r.at[0])
    total_state = st1r[0, 0:64, :]
    total_log = st1r[0, 64:72, :]
    for q in range(1, NX):
        log_q = st1r[q, 64:72, :]
        total_state = jnp.exp(log_q[0:1]) * total_state + st1r[q, 0:64, :]
        total_log = total_log + log_q
    st2s[0:64, :] = total_state
    st2s[64:72, :] = total_log

    def s2(t):
        return remote(st2s, st2r.at[s], s2r.at[s], (lax.rem(s + t, ns), h), 10 + t)

    for t in range(1, ns):

        @pl.when(s + t < ns)
        def _():
            s2(t).start()

    intra(1)
    intra(2)
    intra(3)

    def take(sp, carry):
        remote(st2s, st2r.at[sp], s2r.at[sp], (s, h)).wait_recv()
        factor = jnp.exp(st2r[sp, 64:65, :])
        return factor * carry + st2r[sp, 0:64, :]

    entering = lax.fori_loop(0, s, take, jnp.zeros((64, 128), F32))
    for q in range(NX):
        hs[q] = entering.astype(BF16)
        entering = jnp.exp(st1r[q, 64:65, :]) * entering + st1r[q, 0:64, :]
    held_own = rows(held, 64 * x, 64)
    s3 = []
    for d in range(1, NX):
        xp = mod(x + d, NX)
        c = remote(hs.at[xp], held_own, s3r.at[0], at(s, z, xp), 8)
        c.start()
        s3.append(c)
    held[pl.ds(pl.multiple_of(64 * x, 64), 64), :] = hs[x]

    wait_in(ow.at[pl.ds(0, 96)], sibr.at[1])

    def transpose_ow(k, _):
        at_k = pl.ds(pl.multiple_of(BLK * k, BLK), BLK)
        owt[at_k, :] = ow[:, at_k].T
        return 0

    lax.fori_loop(0, half, transpose_ow, 0)

    wait_in(held.at[pl.ds(0, 192)], s3r.at[0])

    square = jnp.zeros((8, BLK), F32)
    for j in range(NX):
        sl = slice(64 * j, 64 * j + 64)
        y = yv[sl, :] + grow[j : j + 1, :] * dot(held[sl, :], c_cols)
        gated = (y * zsil[sl, :]).astype(BF16).astype(F32)
        square = square + jnp.sum((gated * gated).reshape(8, 8, BLK), axis=0)
        sc[sl, :] = (gated * ptt[sl, 4:5]).astype(BF16)
    sqs[...] = jnp.sum(square, axis=0, keepdims=True)

    def partial(dest):
        return dot(owt[pl.ds(pl.multiple_of(128 * dest, 128), 128), :], sc[...])

    def whole(m):
        return m % 2 == 1 and m < half - 1

    def rs(m, p, direction, to):
        part = pl.ds(0, 128) if whole(m) else pl.ds(32 * p, 32)
        chain = (m - 1) // 2
        sem = rso.at[direction, chain] if whole(m) else rsr.at[direction, chain, p]
        return remote(rs_s.at[direction, m, part], rs_r.at[direction, m, part], sem, to, 1)

    rs_pieces = []

    def rs_start(m, p, direction):
        step = 1 if m % 2 else 2
        rs(m, p, direction, at(s, mod(z + (1 - 2 * direction) * step, nz), x)).start()
        rs_pieces.append(4 if whole(m) else 1)

    def fin_piece(i, xp):
        d = mod(xp - x, NX)
        src = fin_s.at[i, pl.ds(pl.multiple_of(32 * xp, 32), 32)]
        c = remote(src, fin_r.at[i, d], finr.at[d], at(s, mod(z + DELTAS[i], nz), xp), 1)
        c.start()
        rs_pieces.append(1)

    def fin_start(i):
        for d in range(NX):
            if (DELTAS[i], d) != (0, 0):
                fin_piece(i, mod(x + d, NX))

    def own(m, direction):
        return partial(mod(z + (1 - 2 * direction) * m, nz))

    def leaf(m):
        for direction in range(2):
            value = own(m, direction).astype(BF16)
            if m == 1:
                fin_s[2 + direction] = value
                fin_start(2 + direction)
                continue
            rs_s[direction, m] = value
            for p in range(1 if whole(m) else NX):
                if m < half or p // 2 == direction:
                    rs_start(m, p, direction)

    leaf(half)
    leaf(half - 1)
    sq = []
    for d in range(1, nz):
        c = remote(sqs, sqr.at[d - 1], sqrs.at[0], at(s, mod(z + d, nz), x), 9)
        c.start()
        sq.append(c)
    leaf(half - 3)

    mine = partial(z)
    fin_s[4] = mine.astype(BF16)
    sqt_sends = []
    for m in range(half - 2, 0, -2):
        values = [own(m, direction) for direction in range(2)]
        for p in range(NX):
            part = slice(32 * p, 32 * p + 32)
            for direction in range(2):
                if p == 0 and whole(m + 1):
                    rs(m + 1, p, direction, x_up).wait_recv()
                two = m + 2 < half or p // 2 == direction
                both = two and not whole(m + 1)
                if two or not whole(m + 1):
                    wait_in(tok.at[pl.ds(0, 64 if both else 32)], rsr.at[direction, m // 2, p])
                value = values[direction][part] + rs_r[direction, m + 1, part, :].astype(F32)
                if two:
                    value = value + rs_r[direction, m + 2, part, :].astype(F32)
                if m > 2:
                    rs_s[direction, m, part, :] = value.astype(BF16)
                    rs_start(m, p, direction)
                else:
                    fin_s[direction, part, :] = value.astype(BF16)
                    fin_piece(direction, p)
        if m > 3:
            leaf(m - 3)
        if m == half - 2:
            fin_start(4)
            total_sq = sqs[...]
            wait_in(sqr, sqrs.at[0])
            for d in range(1, nz):
                total_sq = total_sq + sqr[d - 1]
            sqt[...] = total_sq
            for d in range(1, NX):
                c = remote(sqt, sqx.at[d - 1], sqtr.at[0], at(s, z, mod(x + d, NX)), 10)
                c.start()
                sqt_sends.append(c)

    wait_in(sqx, sqtr.at[0])
    for d in range(NX):
        if d > 0:
            squares = sqx[d - 1]
        else:
            squares = sqt[...]
        scale = lax.rsqrt(squares / (BLK * nz) + 1e-05)
        if d == 0:
            total = fin_s[4, pl.ds(pl.multiple_of(32 * x, 32), 32), :].astype(F32)
        wait_in(tok.at[pl.ds(0, 160 if d else 128)], finr.at[d])
        for i in (4, 2, 3, 0, 1):
            if (DELTAS[i], d) != (0, 0):
                got = fin_r[i, d].astype(F32)
                total = got if i == 4 else total + got
        from_x = mod(x - d, NX)
        out_ref[:, pl.ds(pl.multiple_of(BLK * from_x, BLK), BLK)] = (total * scale).astype(BF16)

    wait_out(tok.at[pl.ds(0, 32 * (len(first_sends) + sum(ag_pieces)))], 0)
    wait_out(tok.at[pl.ds(0, 32 * sum(rs_pieces))], 1)
    wait_out(zw.at[pl.ds(0, 192)], 2)
    wait_out(zw.at[pl.ds(0, 192)], 3)
    wait_out(ow.at[pl.ds(0, 192)], 4)
    wait_out(par.at[pl.ds(0, NX - 1)], 5)
    wait_out(halo_s, 6)
    wait_out(st1s.at[pl.ds(0, NX - 1)], 7)
    wait_out(hs.at[pl.ds(0, NX - 1)], 8)
    wait_out(sqr, 9)
    wait_out(sqx, 10)
    for t in range(1, ns):

        @pl.when(s + t < ns)
        def _():
            s2(t).wait_send()


def solution(mesh):
    ns = mesh.shape["seq"]
    nz = mesh.shape["head"] // NX
    half = nz // 2

    def body(tokens, z_weight, x_weight, bc_weight, step_weight, x_kernel, bc_kernel, step_bias, log_decay, skip_gain, norm_gain, out_weight):
        width = bc_weight.shape[0]
        vmem = pl.BlockSpec(memory_space=pltpu.VMEM)
        hbm = pl.BlockSpec(memory_space=pltpu.HBM)
        smem = pl.BlockSpec(memory_space=pltpu.SMEM)
        dma = pltpu.SemaphoreType.DMA

        def buf(*shape, dtype=BF16):
            return pltpu.VMEM(shape, dtype)

        out = pl.pallas_call(
            functools.partial(kernel, ns, nz),
            out_shape=jax.ShapeDtypeStruct((32, 4 * BLK), BF16),
            in_specs=[hbm, hbm, hbm, hbm, vmem, vmem, vmem, smem, smem, smem, vmem, hbm],
            out_specs=vmem,
            scratch_shapes=[
                buf(width, BLK),
                buf(256, width),
                buf(256, width),
                buf(width, 256),
                buf(256, width),
                buf(256, width),
                buf(width, 256),
                buf(NX, 24, 128, dtype=F32),
                buf(8, width, dtype=F32),
                buf(128, 512, dtype=F32),
                buf(512, 128, dtype=F32),
                buf(128, 512, dtype=F32),
                buf(512, BLK),
                buf(256, BLK, dtype=F32),
                buf(256, BLK),
                buf(16, 512),
                buf(16, 512),
                buf(128, BLK, dtype=F32),
                buf(16, 128, dtype=F32),
                buf(256, BLK),
                buf(256, BLK, dtype=F32),
                buf(NX, 72, 128, dtype=F32),
                buf(NX, 72, 128, dtype=F32),
                buf(72, 128, dtype=F32),
                buf(ns, 72, 128, dtype=F32),
                buf(NX, 64, 128),
                buf(256, 128),
                buf(1, BLK, dtype=F32),
                buf(nz - 1, 1, BLK, dtype=F32),
                buf(256, BLK),
                buf(1, BLK, dtype=F32),
                buf(NX - 1, 1, BLK, dtype=F32),
                buf(2, half + 1, 128, BLK),
                buf(2, half + 1, 128, BLK),
                buf(5, 128, BLK),
                buf(5, NX, 32, BLK),
                dma((3,)),
                dma((10 + ns,)),
                dma((2, NX)),
                dma((1,)),
                dma((4,)),
                dma((2,)),
                dma((1,)),
                dma((2, half // 2 - 1, NX)),
                dma((2,)),
                dma((1,)),
                dma((1,)),
                dma((ns,)),
                dma((1,)),
                dma((1,)),
                dma((1,)),
                dma((2, half // 2, NX)),
                dma((2, half // 2)),
                dma((NX,)),
            ],
            compiler_params=pltpu.CompilerParams(
                collective_id=0, has_side_effects=True, vmem_limit_bytes=(53 * 1024 + 880) * 1024
            ),
        )(
            tokens.T,
            z_weight.T,
            x_weight.T,
            bc_weight,
            step_weight.T,
            x_kernel,
            bc_kernel,
            step_bias,
            log_decay,
            skip_gain,
            norm_gain.reshape(1, -1),
            out_weight,
        )
        return out.T

    return jax.shard_map(
        body,
        mesh=mesh,
        in_specs=(
            P("seq", "head"),
            P(None, "head"),
            P(None, "head"),
            P(),
            P(None, "head"),
            P(None, "head"),
            P(),
            P("head"),
            P("head"),
            P("head"),
            P("head"),
            P("head", None),
        ),
        out_specs=P("seq", "head"),
        check_vma=False,
    )
```

```python
import functools

import jax
import jax.numpy as jnp
from jax import lax
from jax.experimental import pallas as pl
from jax.experimental.pallas import tpu as pltpu
from jax.sharding import PartitionSpec as P

MESH = pl.DeviceIdType.MESH
F32 = jnp.float32
BF16 = jnp.bfloat16
NX = 4
BLK = 256
DELTAS = (2, -2, 1, -1, 0)
NONE = (((1,), (0,)), ((), ()))
BOTH = (((1,), (1,)), ((), ()))


def dot(a, b, dims=NONE):
    return lax.dot_general(a, b, dims, preferred_element_type=F32)


def kernel(
    ns,
    nz,
    tok_in,
    zw_in,
    xw_in,
    bcw_in,
    sw_in,
    xk_in,
    bck_in,
    bias_in,
    decay_in,
    skip_in,
    gain_in,
    ow_in,
    out_ref,
    tok,
    zw,
    xw,
    bcw,
    bct,
    ow,
    owt,
    par,
    swf,
    pt,
    ptt,
    ct,
    xin,
    zsil,
    xc,
    halo_s,
    halo_r,
    tr,
    bcv,
    wt,
    yv,
    st1s,
    st1r,
    st2s,
    st2r,
    hs,
    held,
    sqs,
    sqr,
    sc,
    sqt,
    sqx,
    rs_s,
    rs_r,
    fin_s,
    fin_r,
    lsem,
    snd,
    p1r,
    p1x,
    wr,
    sibr,
    pr,
    agr,
    ago,
    hsem,
    s1r,
    s2r,
    s3r,
    sqrs,
    sqtr,
    rsr,
    rso,
    finr,
):
    half = nz // 2
    width = 128 * nz
    s = lax.axis_index("seq")
    h = lax.axis_index("head")
    z = h // NX
    x = lax.rem(h, NX)
    core = lax.rem(s, 2)
    block = s * NX + x
    blocks = ns * NX

    def at(s_to, z_to, x_to):
        return (s_to, z_to * NX + x_to)

    def mod(v, n):
        return lax.rem(v + n, n)

    x_up = at(s, z, mod(x + 1, NX))
    x_down = at(s, z, mod(x - 1, NX))
    sibling = (s + 1 - 2 * core, h)
    after = mod(block + 1, blocks)
    before = mod(block - 1, blocks)
    next_dev = at(after // NX, z, lax.rem(after, NX))
    prev_dev = at(before // NX, z, lax.rem(before, NX))

    def remote(src, dst, recv, to, group=0):
        return pltpu.make_async_remote_copy(
            src_ref=src, dst_ref=dst, send_sem=snd.at[group], recv_sem=recv, device_id=to, device_id_type=MESH
        )

    def wait_in(ref, sem):
        remote(ref, ref, sem, sibling).wait_recv()

    def wait_out(ref, group):
        remote(ref, ref, hsem.at[0], sibling, group).wait_send()

    def rows(ref, start, count):
        return ref.at[pl.ds(pl.multiple_of(start, count), count)]

    barrier = pltpu.get_barrier_semaphore()

    def greet(to):
        pl.semaphore_signal(barrier, inc=1, device_id=to, device_id_type=MESH)

    for delta in DELTAS:
        for d in range(NX):
            if (delta, d) != (0, 0):
                greet(at(s, mod(z + delta, nz), mod(x + d, NX)))
    for d in range(1, ns):
        greet((mod(s + d, ns), h))
    greet(next_dev)
    greet(prev_dev)

    own_tok = rows(tok, 128 * z + 32 * x, 32)
    my_cols = pl.ds(pl.multiple_of(BLK * x, BLK), BLK)
    local = [
        pltpu.make_async_copy(tok_in.at[:, my_cols], own_tok, lsem.at[0]),
        pltpu.make_async_copy(bcw_in, bcw, lsem.at[1]),
        pltpu.make_async_copy(zw_in, rows(zw, 64 * x, 64), lsem.at[2]),
        pltpu.make_async_copy(xw_in, rows(xw, 64 * x, 64), lsem.at[2]),
        pltpu.make_async_copy(ow_in, rows(ow, 64 * x, 64), lsem.at[2]),
    ]
    for c in local:
        c.start()

    par[x] = jnp.zeros((24, 128), F32)
    sw = sw_in[...].astype(F32)
    for r in range(nz):
        par[x, r : r + 1, :] = sw[:, 128 * r : 128 * r + 128]
    xk = xk_in[...]
    par[x, 16:20, :] = jnp.concatenate([xk, xk], axis=1)
    gain = gain_in[...].astype(F32)
    par[x, 20:21, :] = jnp.concatenate([gain, gain], axis=1)
    par[x, 21:22, :] = jnp.full((1, 128), bias_in[0], F32)
    par[x, 22:23, :] = jnp.full((1, 128), decay_in[0], F32)
    par[x, 23:24, :] = jnp.full((1, 128), skip_in[0], F32)

    pl.semaphore_wait(barrier, 5 * NX - 1 + (ns - 1) + 2)

    def first(i, d):
        xp = mod(x + d, NX)
        cols = pl.ds(pl.multiple_of(BLK * xp, BLK), BLK)
        to = at(s, mod(z + DELTAS[i], nz), xp)
        return remote(tok_in.at[:, cols], own_tok, p1r.at[i, d] if i < 2 else p1x.at[0], to)

    def first_wait(i, xp):
        d = mod(x - xp, NX)
        ref = rows(tok, 128 * mod(z - DELTAS[i], nz) + 32 * xp, 32)
        remote(ref, ref, p1r.at[i, d] if i < 2 else p1x.at[0], x_up).wait_recv()

    first_sends = [first(i, d) for i in range(5) for d in range(NX) if (DELTAS[i], d) != (0, 0)]
    for c in first_sends:
        c.start()
    small = []
    for d in range(1, NX):
        c = remote(par.at[x], par.at[x], pr.at[0], at(s, z, mod(x + d, NX)), 5)
        c.start()
        small.append(c)

    hr = 32 * core

    def wrow(ref, j):
        return rows(ref, 64 * j + hr, 32)

    half_in = pl.ds(pl.multiple_of(hr, 32), 32)
    wx = []
    for n, (src, buf) in enumerate(((zw_in, zw), (xw_in, xw))):
        up = remote(src.at[half_in], wrow(buf, x), wr.at[0], x_up, 2)
        down = remote(src.at[half_in], wrow(buf, x), wr.at[0], x_down, 2)
        wx.append((up, down))
    wx[1][0].start()
    wx[0][1].start()
    wx[0][0].start()
    wx[1][1].start()

    last = half // 2 - 1

    def ag_rows(k, p, even):
        return (0, 128) if not even and k < last else (32 * p, 32)

    def ag_sem(k, p, direction, even):
        return agr.at[direction, k - 1, p] if even else ago.at[int(k == last)]

    def ag(k, p, direction, even):
        sign = 1 - 2 * direction
        start, count = ag_rows(k, p, even)
        ref = rows(tok, 128 * mod(z - 2 * sign * k, nz) + start, count)
        to = at(s, mod(z + sign * (1 + even), nz), x)
        return remote(ref, ref, ag_sem(k, p, direction, even), to)

    def ag_wait(k, p, direction, even):
        sign = 1 - 2 * direction
        start, count = ag_rows(k, p, even)
        ref = rows(tok, 128 * mod(z - sign * (2 * k + 1 + even), nz) + start, count)
        remote(ref, ref, ag_sem(k, p, direction, even), x_up).wait_recv()

    def ag_has(k, p, direction, even):
        if even:
            return k < last or p // 2 == direction
        return k == last or p == 0

    ag_pieces = []

    def ag_step(k):
        for p in range(NX):
            for direction in range(2):
                if k == 1:
                    first_wait(direction, p)
                else:
                    ag_wait(k - 1, p, direction, 1)
                for even in (1, 0):
                    if ag_has(k, p, direction, even) and (even or k == last):
                        c = ag(k, p, direction, even)
                        c.start()
                        ag_pieces.append(1)
        if k < last:
            for direction in range(2):
                c = ag(k, 0, direction, 0)
                c.start()
                ag_pieces.append(4)

    def transpose_bc(k, _):
        at_k = pl.ds(pl.multiple_of(BLK * k, BLK), BLK)
        bct[:, at_k] = bcw[at_k, :].T
        return 0

    local[1].wait()
    lax.fori_loop(0, half // 2, transpose_bc, 0)
    ag_step(1)
    lax.fori_loop(half // 2, half, transpose_bc, 0)
    wait_in(par.at[pl.ds(0, NX - 1)], pr.at[0])
    swf[...] = jnp.zeros_like(swf)
    for r in range(nz):
        for j in range(NX):
            swf[j : j + 1, 128 * r : 128 * r + 128] = par[j, r : r + 1, :]
    low = lax.broadcasted_iota(jnp.int32, (8, 128), 1) < 64
    pt[...] = jnp.zeros_like(pt)
    for n in range(2):
        pair = jnp.where(low, par[2 * n, 16:24, :], par[2 * n + 1, 16:24, :])
        pt[0:8, 128 * n : 128 * n + 128] = pair
    pt[0:4, 256:512] = bck_in[...]
    ptt[...] = pt[...].T
    for k in range(2, last):
        ag_step(k)

    local[0].wait()
    loaded = zw.at[pl.ds(0, 192)]
    pltpu.make_async_copy(loaded, loaded, lsem.at[2]).wait()
    wait_in(zw.at[pl.ds(0, 128)], wr.at[0])
    down_j = mod(x - 1, NX)
    up_j = mod(x + 1, NX)
    far_j = mod(x + 2, NX)
    fw_up = remote(wrow(xw, down_j), wrow(xw, down_j), wr.at[1], x_up, 2)
    fw_down = remote(wrow(zw, up_j), wrow(zw, up_j), wr.at[1], x_down, 2)
    fw_up.start()
    fw_down.start()
    sib = []
    for n, (buf, j) in enumerate(((zw, down_j), (zw, up_j), (xw, down_j), (xw, up_j), (zw, far_j), (xw, far_j))):
        sib.append(remote(wrow(buf, j), wrow(buf, j), sibr.at[0], sibling, 3))
    for n in range(4):
        sib[n].start()
    if last > 1:
        ag_step(last)

    ow_up = remote(ow_in.at[half_in], wrow(ow, x), wr.at[2], x_up, 4)
    ow_down = remote(ow_in.at[half_in], wrow(ow, x), wr.at[2], x_down, 4)
    ow_up.start()
    ow_down.start()

    wait_in(zw.at[pl.ds(0, 64)], wr.at[1])
    sib[4].start()
    sib[5].start()

    wait_in(tok.at[pl.ds(0, 32 * (3 * NX - 1))], p1x.at[0])
    if last > 1:
        wait_in(tok.at[pl.ds(0, 256 * (last - 1))], ago.at[0])
    wait_in(tok.at[pl.ds(0, 256)], ago.at[1])
    for p in range(NX):
        for direction in range(2):
            if ag_has(last, p, direction, 1):
                ag_wait(last, p, direction, 1)

    tokens = tok[...]
    step_raw = dot(swf[...].astype(BF16), tokens)
    xin[256:512, :] = dot(bct[...], tokens).astype(BF16)
    wait_in(zw.at[pl.ds(0, 192)], sibr.at[0])
    xin[0:256, :] = dot(xw[...], tokens).astype(BF16)

    pick_r = lax.broadcasted_iota(jnp.int32, (16, BLK), 0)
    pick_c = lax.broadcasted_iota(jnp.int32, (16, BLK), 1)
    pick = jnp.where((pick_c == pick_r + BLK - 3) & (pick_r < 3), 1.0, 0.0).astype(BF16)
    halo_s[...] = dot(pick, xin[...], BOTH).astype(BF16)
    halo = remote(halo_s, halo_r, hsem.at[0], next_dev, 6)
    halo.start()

    wait_in(ow.at[pl.ds(0, 64)], wr.at[2])

    def orow(j, part):
        return rows(ow, 64 * j + hr + 16 * part, 16)

    ofw_up = remote(orow(down_j, 0), orow(down_j, 0), wr.at[3], x_up, 4)
    ofw_down = remote(orow(up_j, 1), orow(up_j, 1), wr.at[3], x_down, 4)
    ofw_up.start()
    ofw_down.start()
    osib = []
    for n, j in enumerate((down_j, up_j, far_j)):
        osib.append(remote(wrow(ow, j), wrow(ow, j), sibr.at[1], sibling, 4))
    osib[0].start()
    osib[1].start()

    def heads_col(r):
        col = jnp.concatenate([par[j, r : r + 1, :] for j in range(NX)] + [jnp.zeros((4, 128), F32)], axis=0)
        return jnp.concatenate([col, col], axis=1)

    arg = step_raw + heads_col(21)
    u = jnp.exp(-jnp.abs(arg))
    log1p = jnp.where(u < 0.02, u * (1.0 - u * (0.5 - u * (1.0 / 3.0 - u * (0.25 - u * 0.2)))), jnp.log(1.0 + u))
    step = jnp.maximum(arg, 0.0) + log1p
    rate = -jnp.exp(heads_col(22)) * step
    hi = rate.astype(BF16)
    rest = rate - hi.astype(F32)
    mid_part = rest.astype(BF16)
    lo = (rest - mid_part.astype(F32)).astype(BF16)
    ir = lax.broadcasted_iota(jnp.int32, (BLK, BLK), 0)
    ic = lax.broadcasted_iota(jnp.int32, (BLK, BLK), 1)
    tri = jnp.where(ir <= ic, 1.0, 0.0).astype(BF16)
    cum = dot(hi, tri) + dot(mid_part, tri) + dot(lo, tri)
    end = jnp.broadcast_to(cum[:, BLK - 1 : BLK], (8, BLK))
    tail = jnp.exp(end - cum) * step
    grow = jnp.exp(cum)
    tr[...] = jnp.zeros_like(tr)
    tr[0:8, :] = jnp.log(step) - cum
    col_t = tr[...].T

    z_in = dot(zw[...], tokens).astype(BF16).astype(F32)
    zsil[...] = z_in * jax.nn.sigmoid(z_in)

    halo.wait_recv()
    hrow = halo_r[...].astype(F32)
    k0, k1, k2 = pt[0:1, :], pt[1:2, :], pt[2:3, :]
    h0, h1, h2 = hrow[0:1], hrow[1:2], hrow[2:3]
    first = block > 0
    ct[...] = jnp.zeros_like(ct)
    ct[0:1, :] = jnp.where(first, k0 * h0 + k1 * h1 + k2 * h2, 0.0)
    ct[1:2, :] = jnp.where(first, k0 * h1 + k1 * h2, 0.0)
    ct[2:3, :] = jnp.where(first, k0 * h2, 0.0)
    shift = [jnp.where(ic == ir + d, 1.0, 0.0).astype(BF16) for d in range(1, 4)]
    for r in range(4):
        sl = slice(128 * r, 128 * r + 128)
        piece = xin[sl, :]
        taps = ptt[sl, :]
        total = taps[:, 3:4] * piece.astype(F32)
        for d in range(1, 4):
            total = total + taps[:, 3 - d : 4 - d] * dot(piece, shift[d - 1])
        corr = ct[:, sl].T
        total = jnp.concatenate([total[:, :128] + corr, total[:, 128:]], axis=1)
        total = total * jax.nn.sigmoid(total)
        if r < 2:
            xc[sl, :] = total.astype(BF16)
            for n in range(2):
                j = 2 * r + n
                wt[64 * j : 64 * j + 64, :] = (
                    total[64 * n : 64 * n + 64].astype(BF16).astype(F32) * tail[j : j + 1, :]
                ).astype(BF16)
        elif r == 2:
            b_rows = total.T.astype(BF16)
        else:
            c_cols = total.astype(BF16)

    loc = dot(wt[...], b_rows)
    for j in range(NX):
        st1s[j, 0:64, :] = loc[64 * j : 64 * j + 64]
        st1s[j, 64:72, :] = jnp.broadcast_to(end[j : j + 1, 0:128], (8, 128))
    st1r[x] = st1s[x]
    s1 = []
    for d in range(1, NX):
        xp = mod(x + d, NX)
        c = remote(st1s.at[xp], st1r.at[x], s1r.at[0], at(s, z, xp), 7)
        c.start()
        s1.append(c)

    wait_in(ow.at[pl.ds(0, 32)], wr.at[3])
    osib[2].start()

    gram = dot(b_rows, c_cols)
    lower = ir[:128, :128] <= ic[:128, :128]

    def intra(j):
        row = cum[j : j + 1, :]
        col = col_t[:, j : j + 1]
        d0 = jnp.where(lower, gram[:128, :128] * jnp.exp(row[:, :128] + col[:128]), 0.0).astype(BF16)
        full = (gram[:128, 128:] * jnp.exp(row[:, 128:] + col[:128])).astype(BF16)
        d1 = jnp.where(lower, gram[128:, 128:] * jnp.exp(row[:, 128:] + col[128:]), 0.0).astype(BF16)
        xj = xc[64 * j : 64 * j + 64, :]
        y0 = dot(xj[:, :128], d0)
        y1 = dot(xj, jnp.concatenate([full, d1], axis=0))
        skip = par[j, 23:24, :]
        y = jnp.concatenate([y0, y1], axis=1) + jnp.concatenate([skip, skip], axis=1) * xj.astype(F32)
        yv[64 * j : 64 * j + 64, :] = y

    intra(0)

    wait_in(st1r.at[pl.ds(0, NX - 1)], s1r.at[0])
    total_state = st1r[0, 0:64, :]
    total_log = st1r[0, 64:72, :]
    for q in range(1, NX):
        log_q = st1r[q, 64:72, :]
        total_state = jnp.exp(log_q[0:1]) * total_state + st1r[q, 0:64, :]
        total_log = total_log + log_q
    st2s[0:64, :] = total_state
    st2s[64:72, :] = total_log

    def s2(t):
        return remote(st2s, st2r.at[s], s2r.at[s], (lax.rem(s + t, ns), h), 10 + t)

    for t in range(1, ns):

        @pl.when(s + t < ns)
        def _():
            s2(t).start()

    intra(1)
    intra(2)
    intra(3)

    def take(sp, carry):
        remote(st2s, st2r.at[sp], s2r.at[sp], (s, h)).wait_recv()
        factor = jnp.exp(st2r[sp, 64:65, :])
        return factor * carry + st2r[sp, 0:64, :]

    entering = lax.fori_loop(0, s, take, jnp.zeros((64, 128), F32))
    for q in range(NX):
        hs[q] = entering.astype(BF16)
        entering = jnp.exp(st1r[q, 64:65, :]) * entering + st1r[q, 0:64, :]
    held_own = rows(held, 64 * x, 64)
    s3 = []
    for d in range(1, NX):
        xp = mod(x + d, NX)
        c = remote(hs.at[xp], held_own, s3r.at[0], at(s, z, xp), 8)
        c.start()
        s3.append(c)
    held[pl.ds(pl.multiple_of(64 * x, 64), 64), :] = hs[x]

    wait_in(ow.at[pl.ds(0, 96)], sibr.at[1])

    def transpose_ow(k, _):
        at_k = pl.ds(pl.multiple_of(BLK * k, BLK), BLK)
        owt[at_k, :] = ow[:, at_k].T
        return 0

    lax.fori_loop(0, half, transpose_ow, 0)

    wait_in(held.at[pl.ds(0, 192)], s3r.at[0])

    square = jnp.zeros((8, BLK), F32)
    for j in range(NX):
        sl = slice(64 * j, 64 * j + 64)
        y = yv[sl, :] + grow[j : j + 1, :] * dot(held[sl, :], c_cols)
        gated = (y * zsil[sl, :]).astype(BF16).astype(F32)
        square = square + jnp.sum((gated * gated).reshape(8, 8, BLK), axis=0)
        sc[sl, :] = (gated * ptt[sl, 4:5]).astype(BF16)
    sqs[...] = jnp.sum(square, axis=0, keepdims=True)

    def partial(dest):
        return dot(owt[pl.ds(pl.multiple_of(128 * dest, 128), 128), :], sc[...])

    def whole(m):
        return m % 2 == 1 and m < half - 1

    def rs(m, p, direction, to):
        part = pl.ds(0, 128) if whole(m) else pl.ds(32 * p, 32)
        chain = (m - 1) // 2
        sem = rso.at[direction, chain] if whole(m) else rsr.at[direction, chain, p]
        return remote(rs_s.at[direction, m, part], rs_r.at[direction, m, part], sem, to, 1)

    rs_pieces = []

    def rs_start(m, p, direction):
        step = 1 if m % 2 else 2
        rs(m, p, direction, at(s, mod(z + (1 - 2 * direction) * step, nz), x)).start()
        rs_pieces.append(4 if whole(m) else 1)

    def fin_piece(i, xp):
        d = mod(xp - x, NX)
        src = fin_s.at[i, pl.ds(pl.multiple_of(32 * xp, 32), 32)]
        c = remote(src, fin_r.at[i, d], finr.at[d], at(s, mod(z + DELTAS[i], nz), xp), 1)
        c.start()
        rs_pieces.append(1)

    def fin_start(i):
        for d in range(NX):
            if (DELTAS[i], d) != (0, 0):
                fin_piece(i, mod(x + d, NX))

    def own(m, direction):
        return partial(mod(z + (1 - 2 * direction) * m, nz))

    def leaf(m):
        for direction in range(2):
            value = own(m, direction).astype(BF16)
            if m == 1:
                fin_s[2 + direction] = value
                fin_start(2 + direction)
                continue
            rs_s[direction, m] = value
            for p in range(1 if whole(m) else NX):
                if m < half or p // 2 == direction:
                    rs_start(m, p, direction)

    leaf(half)
    leaf(half - 1)
    sq = []
    for d in range(1, nz):
        c = remote(sqs, sqr.at[d - 1], sqrs.at[0], at(s, mod(z + d, nz), x), 9)
        c.start()
        sq.append(c)
    leaf(half - 3)

    mine = partial(z)
    fin_s[4] = mine.astype(BF16)
    sqt_sends = []
    for m in range(half - 2, 0, -2):
        values = [own(m, direction) for direction in range(2)]
        for p in range(NX):
            part = slice(32 * p, 32 * p + 32)
            for direction in range(2):
                if p == 0 and whole(m + 1):
                    rs(m + 1, p, direction, x_up).wait_recv()
                two = m + 2 < half or p // 2 == direction
                both = two and not whole(m + 1)
                if two or not whole(m + 1):
                    wait_in(tok.at[pl.ds(0, 64 if both else 32)], rsr.at[direction, m // 2, p])
                value = values[direction][part] + rs_r[direction, m + 1, part, :].astype(F32)
                if two:
                    value = value + rs_r[direction, m + 2, part, :].astype(F32)
                if m > 2:
                    rs_s[direction, m, part, :] = value.astype(BF16)
                    rs_start(m, p, direction)
                else:
                    fin_s[direction, part, :] = value.astype(BF16)
                    fin_piece(direction, p)
        if m > 3:
            leaf(m - 3)
        if m == half - 2:
            fin_start(4)
            total_sq = sqs[...]
            wait_in(sqr, sqrs.at[0])
            for d in range(1, nz):
                total_sq = total_sq + sqr[d - 1]
            sqt[...] = total_sq
            for d in range(1, NX):
                c = remote(sqt, sqx.at[d - 1], sqtr.at[0], at(s, z, mod(x + d, NX)), 10)
                c.start()
                sqt_sends.append(c)

    wait_in(sqx, sqtr.at[0])
    for d in range(NX):
        if d > 0:
            squares = sqx[d - 1]
        else:
            squares = sqt[...]
        scale = lax.rsqrt(squares / (BLK * nz) + 1e-05)
        if d == 0:
            total = fin_s[4, pl.ds(pl.multiple_of(32 * x, 32), 32), :].astype(F32)
        wait_in(tok.at[pl.ds(0, 160 if d else 128)], finr.at[d])
        for i in (4, 2, 3, 0, 1):
            if (DELTAS[i], d) != (0, 0):
                got = fin_r[i, d].astype(F32)
                total = got if i == 4 else total + got
        from_x = mod(x - d, NX)
        out_ref[:, pl.ds(pl.multiple_of(BLK * from_x, BLK), BLK)] = (total * scale).astype(BF16)

    wait_out(tok.at[pl.ds(0, 32 * (len(first_sends) + sum(ag_pieces)))], 0)
    wait_out(tok.at[pl.ds(0, 32 * sum(rs_pieces))], 1)
    wait_out(zw.at[pl.ds(0, 192)], 2)
    wait_out(zw.at[pl.ds(0, 192)], 3)
    wait_out(ow.at[pl.ds(0, 192)], 4)
    wait_out(par.at[pl.ds(0, NX - 1)], 5)
    wait_out(halo_s, 6)
    wait_out(st1s.at[pl.ds(0, NX - 1)], 7)
    wait_out(hs.at[pl.ds(0, NX - 1)], 8)
    wait_out(sqr, 9)
    wait_out(sqx, 10)
    for t in range(1, ns):

        @pl.when(s + t < ns)
        def _():
            s2(t).wait_send()


def solution(mesh):
    ns = mesh.shape["seq"]
    nz = mesh.shape["head"] // NX
    half = nz // 2

    def body(tokens, z_weight, x_weight, bc_weight, step_weight, x_kernel, bc_kernel, step_bias, log_decay, skip_gain, norm_gain, out_weight):
        width = bc_weight.shape[0]
        vmem = pl.BlockSpec(memory_space=pltpu.VMEM)
        hbm = pl.BlockSpec(memory_space=pltpu.HBM)
        smem = pl.BlockSpec(memory_space=pltpu.SMEM)
        dma = pltpu.SemaphoreType.DMA

        def pin(value):
            return pltpu.with_memory_space_constraint(value, pltpu.HBM)

        def buf(*shape, dtype=BF16):
            return pltpu.VMEM(shape, dtype)

        out = pl.pallas_call(
            functools.partial(kernel, ns, nz),
            out_shape=pltpu.VMEM((32, 4 * BLK), BF16),
            in_specs=[hbm, hbm, hbm, hbm, vmem, vmem, vmem, smem, smem, smem, vmem, hbm],
            out_specs=vmem,
            scratch_shapes=[
                buf(width, BLK),
                buf(256, width),
                buf(256, width),
                buf(width, 256),
                buf(256, width),
                buf(256, width),
                buf(width, 256),
                buf(NX, 24, 128, dtype=F32),
                buf(8, width, dtype=F32),
                buf(128, 512, dtype=F32),
                buf(512, 128, dtype=F32),
                buf(128, 512, dtype=F32),
                buf(512, BLK),
                buf(256, BLK, dtype=F32),
                buf(256, BLK),
                buf(16, 512),
                buf(16, 512),
                buf(128, BLK, dtype=F32),
                buf(16, 128, dtype=F32),
                buf(256, BLK),
                buf(256, BLK, dtype=F32),
                buf(NX, 72, 128, dtype=F32),
                buf(NX, 72, 128, dtype=F32),
                buf(72, 128, dtype=F32),
                buf(ns, 72, 128, dtype=F32),
                buf(NX, 64, 128),
                buf(256, 128),
                buf(1, BLK, dtype=F32),
                buf(nz - 1, 1, BLK, dtype=F32),
                buf(256, BLK),
                buf(1, BLK, dtype=F32),
                buf(NX - 1, 1, BLK, dtype=F32),
                buf(2, half + 1, 128, BLK),
                buf(2, half + 1, 128, BLK),
                buf(5, 128, BLK),
                buf(5, NX, 32, BLK),
                dma((3,)),
                dma((10 + ns,)),
                dma((2, NX)),
                dma((1,)),
                dma((4,)),
                dma((2,)),
                dma((1,)),
                dma((2, half // 2 - 1, NX)),
                dma((2,)),
                dma((1,)),
                dma((1,)),
                dma((ns,)),
                dma((1,)),
                dma((1,)),
                dma((1,)),
                dma((2, half // 2, NX)),
                dma((2, half // 2)),
                dma((NX,)),
            ],
            compiler_params=pltpu.CompilerParams(
                collective_id=0, has_side_effects=True, vmem_limit_bytes=40 * 1024 * 1024
            ),
        )(
            pin(tokens.T),
            pin(z_weight.T),
            pin(x_weight.T),
            pin(bc_weight),
            step_weight.T,
            x_kernel,
            bc_kernel,
            step_bias,
            log_decay,
            skip_gain,
            norm_gain.reshape(1, -1),
            pin(out_weight),
        )
        return out.T

    return jax.shard_map(
        body,
        mesh=mesh,
        in_specs=(
            P("seq", "head"),
            P(None, "head"),
            P(None, "head"),
            P(),
            P(None, "head"),
            P(None, "head"),
            P(),
            P("head"),
            P("head"),
            P("head"),
            P("head"),
            P("head", None),
        ),
        out_specs=P("seq", "head"),
        check_vma=False,
    )
```

```python
import functools

import jax
import jax.numpy as jnp
from jax import lax
from jax.experimental import pallas as pl
from jax.experimental.pallas import tpu as pltpu
from jax.sharding import PartitionSpec as P

MESH = pl.DeviceIdType.MESH
F32 = jnp.float32
BF16 = jnp.bfloat16
NX = 4
BLK = 256
DELTAS = (2, -2, 1, -1, 0)
NONE = (((1,), (0,)), ((), ()))
BOTH = (((1,), (1,)), ((), ()))


def dot(a, b, dims=NONE):
    return lax.dot_general(a, b, dims, preferred_element_type=F32)


def kernel(
    ns,
    nz,
    tok_in,
    zw_in,
    xw_in,
    bcw_in,
    sw_in,
    xk_in,
    bck_in,
    bias_in,
    decay_in,
    skip_in,
    gain_in,
    ow_in,
    out_ref,
    tok,
    zw,
    xw,
    bcw,
    bct,
    ow,
    owt,
    par,
    swf,
    pt,
    ptt,
    ct,
    xin,
    zsil,
    xc,
    halo_s,
    halo_r,
    tr,
    cv,
    wt,
    yv,
    st1s,
    st1r,
    st2s,
    st2r,
    hs,
    held,
    sqs,
    sqr,
    sc,
    sqt,
    sqx,
    rs_s,
    rs_r,
    fin_s,
    fin_r,
    lsem,
    snd,
    p1r,
    p1x,
    wr,
    sibr,
    pr,
    agr,
    ago,
    hsem,
    s1r,
    s2r,
    s3r,
    sqrs,
    sqtr,
    rsr,
    rso,
    finr,
):
    half = nz // 2
    width = 128 * nz
    s = lax.axis_index("seq")
    h = lax.axis_index("head")
    z = h // NX
    x = lax.rem(h, NX)
    core = lax.rem(s, 2)
    block = s * NX + x
    blocks = ns * NX

    def at(s_to, z_to, x_to):
        return (s_to, z_to * NX + x_to)

    def mod(v, n):
        return lax.rem(v + n, n)

    x_up = at(s, z, mod(x + 1, NX))
    x_down = at(s, z, mod(x - 1, NX))
    sibling = (s + 1 - 2 * core, h)
    after = mod(block + 1, blocks)
    before = mod(block - 1, blocks)
    next_dev = at(after // NX, z, lax.rem(after, NX))
    prev_dev = at(before // NX, z, lax.rem(before, NX))

    def remote(src, dst, recv, to, group=0):
        return pltpu.make_async_remote_copy(
            src_ref=src, dst_ref=dst, send_sem=snd.at[group], recv_sem=recv, device_id=to, device_id_type=MESH
        )

    def wait_in(ref, sem):
        remote(ref, ref, sem, sibling).wait_recv()

    def wait_out(ref, group):
        remote(ref, ref, hsem.at[0], sibling, group).wait_send()

    def rows(ref, start, count):
        return ref.at[pl.ds(pl.multiple_of(start, count), count)]

    barrier = pltpu.get_barrier_semaphore()

    def greet(to):
        pl.semaphore_signal(barrier, inc=1, device_id=to, device_id_type=MESH)

    for delta in DELTAS:
        for d in range(NX):
            if (delta, d) != (0, 0):
                greet(at(s, mod(z + delta, nz), mod(x + d, NX)))
    for d in range(1, ns):
        greet((mod(s + d, ns), h))
    greet(next_dev)
    greet(prev_dev)

    own_tok = rows(tok, 128 * z + 32 * x, 32)
    my_cols = pl.ds(pl.multiple_of(BLK * x, BLK), BLK)
    local = [
        pltpu.make_async_copy(tok_in.at[:, my_cols], own_tok, lsem.at[0]),
        pltpu.make_async_copy(bcw_in, bcw, lsem.at[1]),
        pltpu.make_async_copy(zw_in, rows(zw, 64 * x, 64), lsem.at[2]),
        pltpu.make_async_copy(xw_in, rows(xw, 64 * x, 64), lsem.at[2]),
        pltpu.make_async_copy(ow_in, rows(ow, 64 * x, 64), lsem.at[2]),
    ]
    for c in local:
        c.start()

    par[x] = jnp.zeros((24, 128), F32)
    sw = sw_in[...].astype(F32)
    for r in range(nz):
        par[x, r : r + 1, :] = sw[:, 128 * r : 128 * r + 128]
    xk = xk_in[...]
    par[x, 16:20, :] = jnp.concatenate([xk, xk], axis=1)
    gain = gain_in[...].astype(F32)
    par[x, 20:21, :] = jnp.concatenate([gain, gain], axis=1)
    par[x, 21:22, :] = jnp.full((1, 128), bias_in[0], F32)
    par[x, 22:23, :] = jnp.full((1, 128), decay_in[0], F32)
    par[x, 23:24, :] = jnp.full((1, 128), skip_in[0], F32)

    pl.semaphore_wait(barrier, 5 * NX - 1 + (ns - 1) + 2)

    def first(i, d):
        xp = mod(x + d, NX)
        cols = pl.ds(pl.multiple_of(BLK * xp, BLK), BLK)
        to = at(s, mod(z + DELTAS[i], nz), xp)
        return remote(tok_in.at[:, cols], own_tok, p1r.at[i, d] if i < 2 else p1x.at[0], to)

    def first_wait(i, xp):
        d = mod(x - xp, NX)
        ref = rows(tok, 128 * mod(z - DELTAS[i], nz) + 32 * xp, 32)
        remote(ref, ref, p1r.at[i, d] if i < 2 else p1x.at[0], x_up).wait_recv()

    first_sends = [first(i, d) for i in range(5) for d in range(NX) if (DELTAS[i], d) != (0, 0)]
    for c in first_sends:
        c.start()
    small = []
    for d in range(1, NX):
        c = remote(par.at[x], par.at[x], pr.at[0], at(s, z, mod(x + d, NX)), 5)
        c.start()
        small.append(c)

    hr = 32 * core

    def wrow(ref, j):
        return rows(ref, 64 * j + hr, 32)

    half_in = pl.ds(pl.multiple_of(hr, 32), 32)
    wx = []
    for n, (src, buf) in enumerate(((zw_in, zw), (xw_in, xw))):
        up = remote(src.at[half_in], wrow(buf, x), wr.at[0], x_up, 2)
        down = remote(src.at[half_in], wrow(buf, x), wr.at[0], x_down, 2)
        wx.append((up, down))
    wx[1][0].start()
    wx[0][1].start()
    wx[0][0].start()
    wx[1][1].start()

    last = half // 2 - 1

    def piece(o):
        return mod(x - (0, 1, 3, 2)[o], NX)

    def ag_rows(k, p, even):
        return (0, 128) if not even and k < last else (32 * piece(p), 32)

    def ag_sem(k, p, direction, even):
        return agr.at[direction, k - 1, p] if even else ago.at[int(k == last)]

    def ag(k, p, direction, even):
        sign = 1 - 2 * direction
        start, count = ag_rows(k, p, even)
        ref = rows(tok, 128 * mod(z - 2 * sign * k, nz) + start, count)
        to = at(s, mod(z + sign * (1 + even), nz), x)
        return remote(ref, ref, ag_sem(k, p, direction, even), to)

    def ag_wait(k, p, direction, even):
        sign = 1 - 2 * direction
        start, count = ag_rows(k, p, even)
        ref = rows(tok, 128 * mod(z - sign * (2 * k + 1 + even), nz) + start, count)
        remote(ref, ref, ag_sem(k, p, direction, even), x_up).wait_recv()

    def ag_has(k, p, direction, even):
        if even:
            return k < last or p // 2 == direction
        return k == last or p == 0

    ag_pieces = []

    def ag_step(k):
        for p in range(NX):
            for direction in range(2):
                if k == 1:
                    first_wait(direction, piece(p))
                else:
                    ag_wait(k - 1, p, direction, 1)
                for even in (1, 0):
                    if ag_has(k, p, direction, even) and (even or k == last):
                        c = ag(k, p, direction, even)
                        c.start()
                        ag_pieces.append(1)
        if k < last:
            for direction in range(2):
                c = ag(k, 0, direction, 0)
                c.start()
                ag_pieces.append(4)

    def transpose_bc(k, _):
        at_k = pl.ds(pl.multiple_of(BLK * k, BLK), BLK)
        bct[:, at_k] = bcw[at_k, :].T
        return 0

    local[1].wait()
    lax.fori_loop(0, half // 2, transpose_bc, 0)
    ag_step(1)
    lax.fori_loop(half // 2, half, transpose_bc, 0)
    wait_in(par.at[pl.ds(0, NX - 1)], pr.at[0])
    swf[...] = jnp.zeros_like(swf)
    for r in range(nz):
        for j in range(NX):
            swf[j : j + 1, 128 * r : 128 * r + 128] = par[j, r : r + 1, :]
    low = lax.broadcasted_iota(jnp.int32, (8, 128), 1) < 64
    pt[...] = jnp.zeros_like(pt)
    for n in range(2):
        pair = jnp.where(low, par[2 * n, 16:24, :], par[2 * n + 1, 16:24, :])
        pt[0:8, 128 * n : 128 * n + 128] = pair
    pt[0:4, 256:512] = bck_in[...]
    ptt[...] = pt[...].T
    for k in range(2, last):
        ag_step(k)

    local[0].wait()
    loaded = zw.at[pl.ds(0, 192)]
    pltpu.make_async_copy(loaded, loaded, lsem.at[2]).wait()
    wait_in(zw.at[pl.ds(0, 128)], wr.at[0])
    down_j = mod(x - 1, NX)
    up_j = mod(x + 1, NX)
    far_j = mod(x + 2, NX)
    fw_up = remote(wrow(xw, down_j), wrow(xw, down_j), wr.at[1], x_up, 2)
    fw_down = remote(wrow(zw, up_j), wrow(zw, up_j), wr.at[1], x_down, 2)
    fw_up.start()
    fw_down.start()
    sib = []
    for n, (buf, j) in enumerate(((zw, down_j), (zw, up_j), (xw, down_j), (xw, up_j), (zw, far_j), (xw, far_j))):
        sib.append(remote(wrow(buf, j), wrow(buf, j), sibr.at[0], sibling, 3))
    for n in range(4):
        sib[n].start()
    if last > 1:
        ag_step(last)

    ow_up = remote(ow_in.at[half_in], wrow(ow, x), wr.at[2], x_up, 4)
    ow_down = remote(ow_in.at[half_in], wrow(ow, x), wr.at[2], x_down, 4)
    ow_up.start()
    ow_down.start()

    wait_in(zw.at[pl.ds(0, 64)], wr.at[1])
    sib[4].start()
    sib[5].start()

    wait_in(tok.at[pl.ds(0, 32 * (3 * NX - 1))], p1x.at[0])
    if last > 1:
        wait_in(tok.at[pl.ds(0, 256 * (last - 1))], ago.at[0])
    wait_in(tok.at[pl.ds(0, 256)], ago.at[1])
    for p in range(NX):
        for direction in range(2):
            if ag_has(last, p, direction, 1):
                ag_wait(last, p, direction, 1)

    tokens = tok[...]
    step_raw = dot(swf[...].astype(BF16), tokens)
    xin[256:512, :] = dot(bct[...], tokens).astype(BF16)
    wait_in(zw.at[pl.ds(0, 192)], sibr.at[0])
    xin[0:256, :] = dot(xw[...], tokens).astype(BF16)

    pick_r = lax.broadcasted_iota(jnp.int32, (16, BLK), 0)
    pick_c = lax.broadcasted_iota(jnp.int32, (16, BLK), 1)
    pick = jnp.where((pick_c == pick_r + BLK - 3) & (pick_r < 3), 1.0, 0.0).astype(BF16)
    halo_s[...] = dot(pick, xin[...], BOTH).astype(BF16)
    halo = remote(halo_s, halo_r, hsem.at[0], next_dev, 6)
    halo.start()

    wait_in(ow.at[pl.ds(0, 64)], wr.at[2])

    def orow(j, part):
        return rows(ow, 64 * j + hr + 16 * part, 16)

    ofw_up = remote(orow(down_j, 0), orow(down_j, 0), wr.at[3], x_up, 4)
    ofw_down = remote(orow(up_j, 1), orow(up_j, 1), wr.at[3], x_down, 4)
    ofw_up.start()
    ofw_down.start()
    osib = []
    for n, j in enumerate((down_j, up_j, far_j)):
        osib.append(remote(wrow(ow, j), wrow(ow, j), sibr.at[1], sibling, 4))
    osib[0].start()
    osib[1].start()

    def heads_col(r):
        col = jnp.concatenate([par[j, r : r + 1, :] for j in range(NX)] + [jnp.zeros((4, 128), F32)], axis=0)
        return jnp.concatenate([col, col], axis=1)

    arg = step_raw + heads_col(21)
    u = jnp.exp(-jnp.abs(arg))
    log1p = jnp.where(u < 0.02, u * (1.0 - u * (0.5 - u * (1.0 / 3.0 - u * (0.25 - u * 0.2)))), jnp.log(1.0 + u))
    step = jnp.maximum(arg, 0.0) + log1p
    rate = -jnp.exp(heads_col(22)) * step
    hi = rate.astype(BF16)
    rest = rate - hi.astype(F32)
    mid_part = rest.astype(BF16)
    lo = (rest - mid_part.astype(F32)).astype(BF16)
    ir = lax.broadcasted_iota(jnp.int32, (BLK, BLK), 0)
    ic = lax.broadcasted_iota(jnp.int32, (BLK, BLK), 1)
    tri = jnp.where(ir <= ic, 1.0, 0.0).astype(BF16)
    cum = dot(hi, tri) + dot(mid_part, tri) + dot(lo, tri)
    end = jnp.broadcast_to(cum[:, BLK - 1 : BLK], (8, BLK))
    tail = jnp.exp(end - cum) * step
    grow = jnp.exp(cum)
    tr[...] = jnp.zeros_like(tr)
    tr[0:8, :] = jnp.log(step) - cum
    col_t = tr[...].T

    z_in = dot(zw[...], tokens).astype(BF16).astype(F32)
    zsil[...] = z_in * jax.nn.sigmoid(z_in)

    shift = [jnp.where(ic == ir + d, 1.0, 0.0).astype(BF16) for d in range(1, 4)]
    for r in range(4):
        sl = slice(128 * r, 128 * r + 128)
        chunk = xin[sl, :]
        taps = ptt[sl, :]
        total = taps[:, 3:4] * chunk.astype(F32)
        for d in range(1, 4):
            total = total + taps[:, 3 - d : 4 - d] * dot(chunk, shift[d - 1])
        after_border = total[:, 128:]
        cv[sl, 0:128] = total[:, :128]
        cv[sl, 128:256] = after_border * jax.nn.sigmoid(after_border)
    halo.wait_recv()
    hrow = halo_r[...].astype(F32)
    k0, k1, k2 = pt[0:1, :], pt[1:2, :], pt[2:3, :]
    h0, h1, h2 = hrow[0:1], hrow[1:2], hrow[2:3]
    first = block > 0
    ct[...] = jnp.zeros_like(ct)
    ct[0:1, :] = jnp.where(first, k0 * h0 + k1 * h1 + k2 * h2, 0.0)
    ct[1:2, :] = jnp.where(first, k0 * h1 + k1 * h2, 0.0)
    ct[2:3, :] = jnp.where(first, k0 * h2, 0.0)
    for r in range(4):
        sl = slice(128 * r, 128 * r + 128)
        border = cv[sl, 0:128] + ct[:, sl].T
        total = jnp.concatenate([border * jax.nn.sigmoid(border), cv[sl, 128:256]], axis=1)
        if r < 2:
            xc[sl, :] = total.astype(BF16)
            for n in range(2):
                j = 2 * r + n
                wt[64 * j : 64 * j + 64, :] = (
                    total[64 * n : 64 * n + 64].astype(BF16).astype(F32) * tail[j : j + 1, :]
                ).astype(BF16)
        elif r == 2:
            b_rows = total.T.astype(BF16)
        else:
            c_cols = total.astype(BF16)

    loc = dot(wt[...], b_rows)
    for j in range(NX):
        st1s[j, 0:64, :] = loc[64 * j : 64 * j + 64]
        st1s[j, 64:72, :] = jnp.broadcast_to(end[j : j + 1, 0:128], (8, 128))
    st1r[x] = st1s[x]
    s1 = []
    for d in range(1, NX):
        xp = mod(x + d, NX)
        c = remote(st1s.at[xp], st1r.at[x], s1r.at[0], at(s, z, xp), 7)
        c.start()
        s1.append(c)

    wait_in(ow.at[pl.ds(0, 32)], wr.at[3])
    osib[2].start()

    gram = dot(b_rows, c_cols)
    lower = ir[:128, :128] <= ic[:128, :128]

    def intra(j):
        row = cum[j : j + 1, :]
        col = col_t[:, j : j + 1]
        d0 = jnp.where(lower, gram[:128, :128] * jnp.exp(row[:, :128] + col[:128]), 0.0).astype(BF16)
        full = (gram[:128, 128:] * jnp.exp(row[:, 128:] + col[:128])).astype(BF16)
        d1 = jnp.where(lower, gram[128:, 128:] * jnp.exp(row[:, 128:] + col[128:]), 0.0).astype(BF16)
        xj = xc[64 * j : 64 * j + 64, :]
        y0 = dot(xj[:, :128], d0)
        y1 = dot(xj, jnp.concatenate([full, d1], axis=0))
        skip = par[j, 23:24, :]
        y = jnp.concatenate([y0, y1], axis=1) + jnp.concatenate([skip, skip], axis=1) * xj.astype(F32)
        yv[64 * j : 64 * j + 64, :] = y

    intra(0)

    wait_in(st1r.at[pl.ds(0, NX - 1)], s1r.at[0])
    total_state = st1r[0, 0:64, :]
    total_log = st1r[0, 64:72, :]
    for q in range(1, NX):
        log_q = st1r[q, 64:72, :]
        total_state = jnp.exp(log_q[0:1]) * total_state + st1r[q, 0:64, :]
        total_log = total_log + log_q
    st2s[0:64, :] = total_state
    st2s[64:72, :] = total_log

    def s2(t):
        return remote(st2s, st2r.at[s], s2r.at[s], (lax.rem(s + t, ns), h), 10 + t)

    for t in range(1, ns):

        @pl.when(s + t < ns)
        def _():
            s2(t).start()

    intra(1)
    intra(2)
    intra(3)

    def take(sp, carry):
        remote(st2s, st2r.at[sp], s2r.at[sp], (s, h)).wait_recv()
        factor = jnp.exp(st2r[sp, 64:65, :])
        return factor * carry + st2r[sp, 0:64, :]

    entering = lax.fori_loop(0, s, take, jnp.zeros((64, 128), F32))
    for q in range(NX):
        hs[q] = entering.astype(BF16)
        entering = jnp.exp(st1r[q, 64:65, :]) * entering + st1r[q, 0:64, :]
    held_own = rows(held, 64 * x, 64)
    s3 = []
    for d in range(1, NX):
        xp = mod(x + d, NX)
        c = remote(hs.at[xp], held_own, s3r.at[0], at(s, z, xp), 8)
        c.start()
        s3.append(c)
    held[pl.ds(pl.multiple_of(64 * x, 64), 64), :] = hs[x]

    wait_in(ow.at[pl.ds(0, 96)], sibr.at[1])

    def transpose_ow(k, _):
        at_k = pl.ds(pl.multiple_of(BLK * k, BLK), BLK)
        owt[at_k, :] = ow[:, at_k].T
        return 0

    lax.fori_loop(0, half, transpose_ow, 0)

    wait_in(held.at[pl.ds(0, 192)], s3r.at[0])

    square = jnp.zeros((8, BLK), F32)
    for j in range(NX):
        sl = slice(64 * j, 64 * j + 64)
        y = yv[sl, :] + grow[j : j + 1, :] * dot(held[sl, :], c_cols)
        gated = (y * zsil[sl, :]).astype(BF16).astype(F32)
        square = square + jnp.sum((gated * gated).reshape(8, 8, BLK), axis=0)
        sc[sl, :] = (gated * ptt[sl, 4:5]).astype(BF16)
    sqs[...] = jnp.sum(square, axis=0, keepdims=True)

    def partial(dest):
        return dot(owt[pl.ds(pl.multiple_of(128 * dest, 128), 128), :], sc[...])

    def whole(m):
        return m % 2 == 1 and m < half - 1

    def rs(m, p, direction, to):
        part = pl.ds(0, 128) if whole(m) else pl.ds(32 * p, 32)
        chain = (m - 1) // 2
        sem = rso.at[direction, chain] if whole(m) else rsr.at[direction, chain, p]
        return remote(rs_s.at[direction, m, part], rs_r.at[direction, m, part], sem, to, 1)

    rs_pieces = []

    def rs_start(m, p, direction):
        step = 1 if m % 2 else 2
        rs(m, p, direction, at(s, mod(z + (1 - 2 * direction) * step, nz), x)).start()
        rs_pieces.append(4 if whole(m) else 1)

    def fin_piece(i, xp):
        d = mod(xp - x, NX)
        src = fin_s.at[i, pl.ds(pl.multiple_of(32 * xp, 32), 32)]
        c = remote(src, fin_r.at[i, d], finr.at[d], at(s, mod(z + DELTAS[i], nz), xp), 1)
        c.start()
        rs_pieces.append(1)

    def fin_start(i):
        for d in range(NX):
            if (DELTAS[i], d) != (0, 0):
                fin_piece(i, mod(x + d, NX))

    def own(m, direction):
        return partial(mod(z + (1 - 2 * direction) * m, nz))

    def leaf(m):
        for direction in range(2):
            value = own(m, direction).astype(BF16)
            if m == 1:
                fin_s[2 + direction] = value
                fin_start(2 + direction)
                continue
            rs_s[direction, m] = value
            for p in range(1 if whole(m) else NX):
                if m < half or p // 2 == direction:
                    rs_start(m, p, direction)

    leaf(half)
    leaf(half - 1)
    sq = []
    for d in range(1, nz):
        c = remote(sqs, sqr.at[d - 1], sqrs.at[0], at(s, mod(z + d, nz), x), 9)
        c.start()
        sq.append(c)
    leaf(half - 3)

    mine = partial(z)
    fin_s[4] = mine.astype(BF16)
    sqt_sends = []
    for m in range(half - 2, 0, -2):
        values = [own(m, direction) for direction in range(2)]
        for p in range(NX):
            part = slice(32 * p, 32 * p + 32)
            for direction in range(2):
                if p == 0 and whole(m + 1):
                    rs(m + 1, p, direction, x_up).wait_recv()
                two = m + 2 < half or p // 2 == direction
                both = two and not whole(m + 1)
                if two or not whole(m + 1):
                    wait_in(tok.at[pl.ds(0, 64 if both else 32)], rsr.at[direction, m // 2, p])
                value = values[direction][part] + rs_r[direction, m + 1, part, :].astype(F32)
                if two:
                    value = value + rs_r[direction, m + 2, part, :].astype(F32)
                if m > 2:
                    rs_s[direction, m, part, :] = value.astype(BF16)
                    rs_start(m, p, direction)
                else:
                    fin_s[direction, part, :] = value.astype(BF16)
                    fin_piece(direction, p)
        if m > 3:
            leaf(m - 3)
        if m == half - 2:
            fin_start(4)
            total_sq = sqs[...]
            wait_in(sqr, sqrs.at[0])
            for d in range(1, nz):
                total_sq = total_sq + sqr[d - 1]
            sqt[...] = total_sq
            for d in range(1, NX):
                c = remote(sqt, sqx.at[d - 1], sqtr.at[0], at(s, z, mod(x + d, NX)), 10)
                c.start()
                sqt_sends.append(c)

    wait_in(sqx, sqtr.at[0])
    for d in range(NX):
        if d > 0:
            squares = sqx[d - 1]
        else:
            squares = sqt[...]
        scale = lax.rsqrt(squares / (BLK * nz) + 1e-05)
        if d == 0:
            total = fin_s[4, pl.ds(pl.multiple_of(32 * x, 32), 32), :].astype(F32)
        wait_in(tok.at[pl.ds(0, 160 if d else 128)], finr.at[d])
        for i in (4, 2, 3, 0, 1):
            if (DELTAS[i], d) != (0, 0):
                got = fin_r[i, d].astype(F32)
                total = got if i == 4 else total + got
        from_x = mod(x - d, NX)
        out_ref[:, pl.ds(pl.multiple_of(BLK * from_x, BLK), BLK)] = (total * scale).astype(BF16)

    wait_out(tok.at[pl.ds(0, 32 * (len(first_sends) + sum(ag_pieces)))], 0)
    wait_out(tok.at[pl.ds(0, 32 * sum(rs_pieces))], 1)
    wait_out(zw.at[pl.ds(0, 192)], 2)
    wait_out(zw.at[pl.ds(0, 192)], 3)
    wait_out(ow.at[pl.ds(0, 192)], 4)
    wait_out(par.at[pl.ds(0, NX - 1)], 5)
    wait_out(halo_s, 6)
    wait_out(st1s.at[pl.ds(0, NX - 1)], 7)
    wait_out(hs.at[pl.ds(0, NX - 1)], 8)
    wait_out(sqr, 9)
    wait_out(sqx, 10)
    for t in range(1, ns):

        @pl.when(s + t < ns)
        def _():
            s2(t).wait_send()


def solution(mesh):
    ns = mesh.shape["seq"]
    nz = mesh.shape["head"] // NX
    half = nz // 2

    def body(tokens, z_weight, x_weight, bc_weight, step_weight, x_kernel, bc_kernel, step_bias, log_decay, skip_gain, norm_gain, out_weight):
        width = bc_weight.shape[0]
        vmem = pl.BlockSpec(memory_space=pltpu.VMEM)
        hbm = pl.BlockSpec(memory_space=pltpu.HBM)
        smem = pl.BlockSpec(memory_space=pltpu.SMEM)
        dma = pltpu.SemaphoreType.DMA

        def pin(value):
            return pltpu.with_memory_space_constraint(value, pltpu.HBM)

        def buf(*shape, dtype=BF16):
            return pltpu.VMEM(shape, dtype)

        out = pl.pallas_call(
            functools.partial(kernel, ns, nz),
            out_shape=pltpu.VMEM((32, 4 * BLK), BF16),
            in_specs=[hbm, hbm, hbm, hbm, vmem, vmem, vmem, smem, smem, smem, vmem, hbm],
            out_specs=vmem,
            scratch_shapes=[
                buf(width, BLK),
                buf(256, width),
                buf(256, width),
                buf(width, 256),
                buf(256, width),
                buf(256, width),
                buf(width, 256),
                buf(NX, 24, 128, dtype=F32),
                buf(8, width, dtype=F32),
                buf(128, 512, dtype=F32),
                buf(512, 128, dtype=F32),
                buf(128, 512, dtype=F32),
                buf(512, BLK),
                buf(256, BLK, dtype=F32),
                buf(256, BLK),
                buf(16, 512),
                buf(16, 512),
                buf(128, BLK, dtype=F32),
                buf(512, BLK, dtype=F32),
                buf(256, BLK),
                buf(256, BLK, dtype=F32),
                buf(NX, 72, 128, dtype=F32),
                buf(NX, 72, 128, dtype=F32),
                buf(72, 128, dtype=F32),
                buf(ns, 72, 128, dtype=F32),
                buf(NX, 64, 128),
                buf(256, 128),
                buf(1, BLK, dtype=F32),
                buf(nz - 1, 1, BLK, dtype=F32),
                buf(256, BLK),
                buf(1, BLK, dtype=F32),
                buf(NX - 1, 1, BLK, dtype=F32),
                buf(2, half + 1, 128, BLK),
                buf(2, half + 1, 128, BLK),
                buf(5, 128, BLK),
                buf(5, NX, 32, BLK),
                dma((3,)),
                dma((10 + ns,)),
                dma((2, NX)),
                dma((1,)),
                dma((4,)),
                dma((2,)),
                dma((1,)),
                dma((2, half // 2 - 1, NX)),
                dma((2,)),
                dma((1,)),
                dma((1,)),
                dma((ns,)),
                dma((1,)),
                dma((1,)),
                dma((1,)),
                dma((2, half // 2, NX)),
                dma((2, half // 2)),
                dma((NX,)),
            ],
            compiler_params=pltpu.CompilerParams(
                collective_id=0, has_side_effects=True, vmem_limit_bytes=40 * 1024 * 1024
            ),
        )(
            pin(tokens.T),
            pin(z_weight.T),
            pin(x_weight.T),
            pin(bc_weight),
            step_weight.T,
            x_kernel,
            bc_kernel,
            step_bias,
            log_decay,
            skip_gain,
            norm_gain.reshape(1, -1),
            pin(out_weight),
        )
        return out.T

    return jax.shard_map(
        body,
        mesh=mesh,
        in_specs=(
            P("seq", "head"),
            P(None, "head"),
            P(None, "head"),
            P(),
            P(None, "head"),
            P(None, "head"),
            P(),
            P("head"),
            P("head"),
            P("head"),
            P("head"),
            P("head", None),
        ),
        out_specs=P("seq", "head"),
        check_vma=False,
    )
```

```python
import functools

import jax
import jax.numpy as jnp
from jax import lax
from jax.experimental import pallas as pl
from jax.experimental.pallas import tpu as pltpu
from jax.sharding import PartitionSpec as P

MESH = pl.DeviceIdType.MESH
F32 = jnp.float32
BF16 = jnp.bfloat16
NX = 4
BLK = 256
DELTAS = (2, -2, 1, -1, 0)
NONE = (((1,), (0,)), ((), ()))
BOTH = (((1,), (1,)), ((), ()))


def dot(a, b, dims=NONE):
    return lax.dot_general(a, b, dims, preferred_element_type=F32)


def kernel(
    ns,
    nz,
    tok_in,
    zw_in,
    xw_in,
    bcw_in,
    sw_in,
    xk_in,
    bck_in,
    bias_in,
    decay_in,
    skip_in,
    gain_in,
    ow_in,
    out_ref,
    tok,
    zw,
    xw,
    bcw,
    bct,
    ow,
    owt,
    par,
    swf,
    pt,
    ptt,
    ct,
    xin,
    zsil,
    xc,
    halo_s,
    halo_r,
    tr,
    cv,
    wt,
    yv,
    st1s,
    st1r,
    st2s,
    st2r,
    hs,
    held,
    sqs,
    sqr,
    sc,
    sqt,
    sqx,
    rs_s,
    rs_r,
    fin_s,
    fin_r,
    lsem,
    snd,
    p1r,
    p1x,
    wr,
    sibr,
    pr,
    agr,
    ago,
    hsem,
    s1r,
    s2r,
    s3r,
    sqrs,
    sqtr,
    rsr,
    rso,
    finr,
):
    half = nz // 2
    width = 128 * nz
    s = lax.axis_index("seq")
    h = lax.axis_index("head")
    z = h // NX
    x = lax.rem(h, NX)
    core = lax.rem(s, 2)
    block = s * NX + x
    blocks = ns * NX

    def at(s_to, z_to, x_to):
        return (s_to, z_to * NX + x_to)

    def mod(v, n):
        return lax.rem(v + n, n)

    x_up = at(s, z, mod(x + 1, NX))
    x_down = at(s, z, mod(x - 1, NX))
    sibling = (s + 1 - 2 * core, h)
    after = mod(block + 1, blocks)
    before = mod(block - 1, blocks)
    next_dev = at(after // NX, z, lax.rem(after, NX))
    prev_dev = at(before // NX, z, lax.rem(before, NX))

    def remote(src, dst, recv, to, group=0):
        return pltpu.make_async_remote_copy(
            src_ref=src, dst_ref=dst, send_sem=snd.at[group], recv_sem=recv, device_id=to, device_id_type=MESH
        )

    def wait_in(ref, sem):
        remote(ref, ref, sem, sibling).wait_recv()

    def wait_out(ref, group):
        remote(ref, ref, hsem.at[0], sibling, group).wait_send()

    def rows(ref, start, count):
        return ref.at[pl.ds(pl.multiple_of(start, count), count)]

    barrier = pltpu.get_barrier_semaphore()

    def greet(to):
        pl.semaphore_signal(barrier, inc=1, device_id=to, device_id_type=MESH)

    for delta in DELTAS:
        for d in range(NX):
            if (delta, d) != (0, 0):
                greet(at(s, mod(z + delta, nz), mod(x + d, NX)))
    for d in range(1, ns):
        greet((mod(s + d, ns), h))
    greet(next_dev)
    greet(prev_dev)

    own_tok = rows(tok, 128 * z + 32 * x, 32)
    my_cols = pl.ds(pl.multiple_of(BLK * x, BLK), BLK)
    local = [
        pltpu.make_async_copy(tok_in.at[:, my_cols], own_tok, lsem.at[0]),
        pltpu.make_async_copy(bcw_in, bcw, lsem.at[1]),
        pltpu.make_async_copy(zw_in, rows(zw, 64 * x, 64), lsem.at[2]),
        pltpu.make_async_copy(xw_in, rows(xw, 64 * x, 64), lsem.at[2]),
        pltpu.make_async_copy(ow_in, rows(ow, 64 * x, 64), lsem.at[2]),
    ]
    for c in local:
        c.start()

    par[x] = jnp.zeros((24, 128), F32)
    sw = sw_in[...].astype(F32)
    for r in range(nz):
        par[x, r : r + 1, :] = sw[:, 128 * r : 128 * r + 128]
    xk = xk_in[...]
    par[x, 16:20, :] = jnp.concatenate([xk, xk], axis=1)
    gain = gain_in[...].astype(F32)
    par[x, 20:21, :] = jnp.concatenate([gain, gain], axis=1)
    par[x, 21:22, :] = jnp.full((1, 128), bias_in[0], F32)
    par[x, 22:23, :] = jnp.full((1, 128), decay_in[0], F32)
    par[x, 23:24, :] = jnp.full((1, 128), skip_in[0], F32)

    pl.semaphore_wait(barrier, 5 * NX - 1 + (ns - 1) + 2)

    def first(i, d):
        xp = mod(x + d, NX)
        cols = pl.ds(pl.multiple_of(BLK * xp, BLK), BLK)
        to = at(s, mod(z + DELTAS[i], nz), xp)
        return remote(tok_in.at[:, cols], own_tok, p1r.at[i, d] if i < 2 else p1x.at[0], to)

    def first_wait(i, xp):
        d = mod(x - xp, NX)
        ref = rows(tok, 128 * mod(z - DELTAS[i], nz) + 32 * xp, 32)
        remote(ref, ref, p1r.at[i, d] if i < 2 else p1x.at[0], x_up).wait_recv()

    first_sends = [first(i, d) for i in range(5) for d in range(NX) if (DELTAS[i], d) != (0, 0)]
    for c in first_sends:
        c.start()
    small = []
    for d in range(1, NX):
        c = remote(par.at[x], par.at[x], pr.at[0], at(s, z, mod(x + d, NX)), 5)
        c.start()
        small.append(c)

    hr = 32 * core

    def wrow(ref, j):
        return rows(ref, 64 * j + hr, 32)

    half_in = pl.ds(pl.multiple_of(hr, 32), 32)
    wx = []
    for n, (src, buf) in enumerate(((zw_in, zw), (xw_in, xw))):
        up = remote(src.at[half_in], wrow(buf, x), wr.at[0], x_up, 2)
        down = remote(src.at[half_in], wrow(buf, x), wr.at[0], x_down, 2)
        wx.append((up, down))
    wx[1][0].start()
    wx[0][1].start()
    wx[0][0].start()
    wx[1][1].start()

    ow_up = remote(ow_in.at[half_in], wrow(ow, x), wr.at[2], x_up, 4)
    ow_down = remote(ow_in.at[half_in], wrow(ow, x), wr.at[2], x_down, 4)
    ow_up.start()
    ow_down.start()

    last = half // 2 - 1

    def piece(o):
        return mod(x - (0, 1, 3, 2)[o], NX)

    def ag_rows(k, p, even):
        return (0, 128) if not even and k < last else (32 * piece(p), 32)

    def ag_sem(k, p, direction, even):
        return agr.at[direction, k - 1, p] if even else ago.at[int(k == last)]

    def ag(k, p, direction, even):
        sign = 1 - 2 * direction
        start, count = ag_rows(k, p, even)
        ref = rows(tok, 128 * mod(z - 2 * sign * k, nz) + start, count)
        to = at(s, mod(z + sign * (1 + even), nz), x)
        return remote(ref, ref, ag_sem(k, p, direction, even), to)

    def ag_wait(k, p, direction, even):
        sign = 1 - 2 * direction
        start, count = ag_rows(k, p, even)
        ref = rows(tok, 128 * mod(z - sign * (2 * k + 1 + even), nz) + start, count)
        remote(ref, ref, ag_sem(k, p, direction, even), x_up).wait_recv()

    def ag_has(k, p, direction, even):
        if even:
            return k < last or p // 2 == direction
        return k == last or p == 0

    ag_pieces = []

    def ag_step(k):
        for p in range(NX):
            for direction in range(2):
                if k == 1:
                    first_wait(direction, piece(p))
                else:
                    ag_wait(k - 1, p, direction, 1)
                for even in (1, 0):
                    if ag_has(k, p, direction, even) and (even or k == last):
                        c = ag(k, p, direction, even)
                        c.start()
                        ag_pieces.append(1)
        if k < last:
            for direction in range(2):
                c = ag(k, 0, direction, 0)
                c.start()
                ag_pieces.append(4)

    def transpose_bc(k, _):
        at_k = pl.ds(pl.multiple_of(BLK * k, BLK), BLK)
        bct[:, at_k] = bcw[at_k, :].T
        return 0

    local[1].wait()
    lax.fori_loop(0, half // 2, transpose_bc, 0)
    ag_step(1)
    lax.fori_loop(half // 2, half, transpose_bc, 0)
    wait_in(par.at[pl.ds(0, NX - 1)], pr.at[0])
    swf[...] = jnp.zeros_like(swf)
    for r in range(nz):
        for j in range(NX):
            swf[j : j + 1, 128 * r : 128 * r + 128] = par[j, r : r + 1, :]
    low = lax.broadcasted_iota(jnp.int32, (8, 128), 1) < 64
    pt[...] = jnp.zeros_like(pt)
    for n in range(2):
        pair = jnp.where(low, par[2 * n, 16:24, :], par[2 * n + 1, 16:24, :])
        pt[0:8, 128 * n : 128 * n + 128] = pair
    pt[0:4, 256:512] = bck_in[...]
    ptt[...] = pt[...].T
    for k in range(2, last):
        ag_step(k)

    local[0].wait()
    loaded = zw.at[pl.ds(0, 192)]
    pltpu.make_async_copy(loaded, loaded, lsem.at[2]).wait()
    wait_in(zw.at[pl.ds(0, 128)], wr.at[0])
    down_j = mod(x - 1, NX)
    up_j = mod(x + 1, NX)
    far_j = mod(x + 2, NX)
    fw_up = remote(wrow(xw, down_j), wrow(xw, down_j), wr.at[1], x_up, 2)
    fw_down = remote(wrow(zw, up_j), wrow(zw, up_j), wr.at[1], x_down, 2)
    fw_up.start()
    fw_down.start()
    sib = []
    for n, (buf, j) in enumerate(((zw, down_j), (zw, up_j), (xw, down_j), (xw, up_j), (zw, far_j), (xw, far_j))):
        sib.append(remote(wrow(buf, j), wrow(buf, j), sibr.at[0], sibling, 3))
    for n in range(4):
        sib[n].start()
    if last > 1:
        ag_step(last)

    wait_in(zw.at[pl.ds(0, 64)], wr.at[1])
    sib[4].start()
    sib[5].start()

    wait_in(ow.at[pl.ds(0, 64)], wr.at[2])

    def orow(j, part):
        return rows(ow, 64 * j + hr + 16 * part, 16)

    ofw_up = remote(orow(down_j, 0), orow(down_j, 0), wr.at[3], x_up, 4)
    ofw_down = remote(orow(up_j, 1), orow(up_j, 1), wr.at[3], x_down, 4)
    ofw_up.start()
    ofw_down.start()
    osib = []
    for n, j in enumerate((down_j, up_j, far_j)):
        osib.append(remote(wrow(ow, j), wrow(ow, j), sibr.at[1], sibling, 4))
    osib[0].start()
    osib[1].start()

    wait_in(tok.at[pl.ds(0, 32 * (3 * NX - 1))], p1x.at[0])
    if last > 1:
        wait_in(tok.at[pl.ds(0, 256 * (last - 1))], ago.at[0])
    wait_in(tok.at[pl.ds(0, 256)], ago.at[1])
    for p in range(NX):
        for direction in range(2):
            if ag_has(last, p, direction, 1):
                ag_wait(last, p, direction, 1)

    tokens = tok[...]
    step_raw = dot(swf[...].astype(BF16), tokens)
    xin[256:512, :] = dot(bct[...], tokens).astype(BF16)
    wait_in(zw.at[pl.ds(0, 192)], sibr.at[0])
    xin[0:256, :] = dot(xw[...], tokens).astype(BF16)

    pick_r = lax.broadcasted_iota(jnp.int32, (16, BLK), 0)
    pick_c = lax.broadcasted_iota(jnp.int32, (16, BLK), 1)
    pick = jnp.where((pick_c == pick_r + BLK - 3) & (pick_r < 3), 1.0, 0.0).astype(BF16)
    halo_s[...] = dot(pick, xin[...], BOTH).astype(BF16)
    halo = remote(halo_s, halo_r, hsem.at[0], next_dev, 6)
    halo.start()

    def heads_col(r):
        col = jnp.concatenate([par[j, r : r + 1, :] for j in range(NX)] + [jnp.zeros((4, 128), F32)], axis=0)
        return jnp.concatenate([col, col], axis=1)

    arg = step_raw + heads_col(21)
    u = jnp.exp(-jnp.abs(arg))
    log1p = jnp.where(u < 0.02, u * (1.0 - u * (0.5 - u * (1.0 / 3.0 - u * (0.25 - u * 0.2)))), jnp.log(1.0 + u))
    step = jnp.maximum(arg, 0.0) + log1p
    rate = -jnp.exp(heads_col(22)) * step
    hi = rate.astype(BF16)
    rest = rate - hi.astype(F32)
    mid_part = rest.astype(BF16)
    lo = (rest - mid_part.astype(F32)).astype(BF16)
    ir = lax.broadcasted_iota(jnp.int32, (BLK, BLK), 0)
    ic = lax.broadcasted_iota(jnp.int32, (BLK, BLK), 1)
    tri = jnp.where(ir <= ic, 1.0, 0.0).astype(BF16)
    cum = dot(hi, tri) + dot(mid_part, tri) + dot(lo, tri)
    end = jnp.broadcast_to(cum[:, BLK - 1 : BLK], (8, BLK))
    tail = jnp.exp(end - cum) * step
    grow = jnp.exp(cum)
    tr[...] = jnp.zeros_like(tr)
    tr[0:8, :] = jnp.log(step) - cum
    col_t = tr[...].T

    z_in = dot(zw[...], tokens).astype(BF16).astype(F32)
    zsil[...] = z_in * jax.nn.sigmoid(z_in)

    shift = [jnp.where(ic == ir + d, 1.0, 0.0).astype(BF16) for d in range(1, 4)]
    for r in range(4):
        sl = slice(128 * r, 128 * r + 128)
        chunk = xin[sl, :]
        taps = ptt[sl, :]
        total = taps[:, 3:4] * chunk.astype(F32)
        for d in range(1, 4):
            total = total + taps[:, 3 - d : 4 - d] * dot(chunk, shift[d - 1])
        after_border = total[:, 128:]
        cv[sl, 0:128] = total[:, :128]
        cv[sl, 128:256] = after_border * jax.nn.sigmoid(after_border)
    halo.wait_recv()
    hrow = halo_r[...].astype(F32)
    k0, k1, k2 = pt[0:1, :], pt[1:2, :], pt[2:3, :]
    h0, h1, h2 = hrow[0:1], hrow[1:2], hrow[2:3]
    first = block > 0
    ct[...] = jnp.zeros_like(ct)
    ct[0:1, :] = jnp.where(first, k0 * h0 + k1 * h1 + k2 * h2, 0.0)
    ct[1:2, :] = jnp.where(first, k0 * h1 + k1 * h2, 0.0)
    ct[2:3, :] = jnp.where(first, k0 * h2, 0.0)
    for r in range(4):
        sl = slice(128 * r, 128 * r + 128)
        border = cv[sl, 0:128] + ct[:, sl].T
        total = jnp.concatenate([border * jax.nn.sigmoid(border), cv[sl, 128:256]], axis=1)
        if r < 2:
            xc[sl, :] = total.astype(BF16)
            for n in range(2):
                j = 2 * r + n
                wt[64 * j : 64 * j + 64, :] = (
                    total[64 * n : 64 * n + 64].astype(BF16).astype(F32) * tail[j : j + 1, :]
                ).astype(BF16)
        elif r == 2:
            b_rows = total.T.astype(BF16)
        else:
            c_cols = total.astype(BF16)

    loc = dot(wt[...], b_rows)
    for j in range(NX):
        st1s[j, 0:64, :] = loc[64 * j : 64 * j + 64]
        st1s[j, 64:72, :] = jnp.broadcast_to(end[j : j + 1, 0:128], (8, 128))
    st1r[x] = st1s[x]
    s1 = []
    for d in range(1, NX):
        xp = mod(x + d, NX)
        c = remote(st1s.at[xp], st1r.at[x], s1r.at[0], at(s, z, xp), 7)
        c.start()
        s1.append(c)

    wait_in(ow.at[pl.ds(0, 32)], wr.at[3])
    osib[2].start()

    gram = dot(b_rows, c_cols)
    lower = ir[:128, :128] <= ic[:128, :128]

    def intra(j):
        row = cum[j : j + 1, :]
        col = col_t[:, j : j + 1]
        d0 = jnp.where(lower, gram[:128, :128] * jnp.exp(row[:, :128] + col[:128]), 0.0).astype(BF16)
        full = (gram[:128, 128:] * jnp.exp(row[:, 128:] + col[:128])).astype(BF16)
        d1 = jnp.where(lower, gram[128:, 128:] * jnp.exp(row[:, 128:] + col[128:]), 0.0).astype(BF16)
        xj = xc[64 * j : 64 * j + 64, :]
        y0 = dot(xj[:, :128], d0)
        y1 = dot(xj, jnp.concatenate([full, d1], axis=0))
        skip = par[j, 23:24, :]
        y = jnp.concatenate([y0, y1], axis=1) + jnp.concatenate([skip, skip], axis=1) * xj.astype(F32)
        yv[64 * j : 64 * j + 64, :] = y

    intra(0)

    wait_in(st1r.at[pl.ds(0, NX - 1)], s1r.at[0])
    total_state = st1r[0, 0:64, :]
    total_log = st1r[0, 64:72, :]
    for q in range(1, NX):
        log_q = st1r[q, 64:72, :]
        total_state = jnp.exp(log_q[0:1]) * total_state + st1r[q, 0:64, :]
        total_log = total_log + log_q
    st2s[0:64, :] = total_state
    st2s[64:72, :] = total_log

    def s2(t):
        return remote(st2s, st2r.at[s], s2r.at[s], (lax.rem(s + t, ns), h), 10 + t)

    for t in range(1, ns):

        @pl.when(s + t < ns)
        def _():
            s2(t).start()

    intra(1)
    intra(2)
    intra(3)

    def take(sp, carry):
        remote(st2s, st2r.at[sp], s2r.at[sp], (s, h)).wait_recv()
        factor = jnp.exp(st2r[sp, 64:65, :])
        return factor * carry + st2r[sp, 0:64, :]

    entering = lax.fori_loop(0, s, take, jnp.zeros((64, 128), F32))
    for q in range(NX):
        hs[q] = entering.astype(BF16)
        entering = jnp.exp(st1r[q, 64:65, :]) * entering + st1r[q, 0:64, :]
    held_own = rows(held, 64 * x, 64)
    s3 = []
    for d in range(1, NX):
        xp = mod(x + d, NX)
        c = remote(hs.at[xp], held_own, s3r.at[0], at(s, z, xp), 8)
        c.start()
        s3.append(c)
    held[pl.ds(pl.multiple_of(64 * x, 64), 64), :] = hs[x]

    wait_in(ow.at[pl.ds(0, 96)], sibr.at[1])

    def transpose_ow(k, _):
        at_k = pl.ds(pl.multiple_of(BLK * k, BLK), BLK)
        owt[at_k, :] = ow[:, at_k].T
        return 0

    lax.fori_loop(0, half, transpose_ow, 0)

    wait_in(held.at[pl.ds(0, 192)], s3r.at[0])

    square = jnp.zeros((8, BLK), F32)
    for j in range(NX):
        sl = slice(64 * j, 64 * j + 64)
        y = yv[sl, :] + grow[j : j + 1, :] * dot(held[sl, :], c_cols)
        gated = (y * zsil[sl, :]).astype(BF16).astype(F32)
        square = square + jnp.sum((gated * gated).reshape(8, 8, BLK), axis=0)
        sc[sl, :] = (gated * ptt[sl, 4:5]).astype(BF16)
    sqs[...] = jnp.sum(square, axis=0, keepdims=True)

    def partial(dest):
        return dot(owt[pl.ds(pl.multiple_of(128 * dest, 128), 128), :], sc[...])

    def whole(m):
        return m % 2 == 1 and m < half - 1

    def rs(m, p, direction, to):
        part = pl.ds(0, 128) if whole(m) else pl.ds(32 * p, 32)
        chain = (m - 1) // 2
        sem = rso.at[direction, chain] if whole(m) else rsr.at[direction, chain, p]
        return remote(rs_s.at[direction, m, part], rs_r.at[direction, m, part], sem, to, 1)

    rs_pieces = []

    def rs_start(m, p, direction):
        step = 1 if m % 2 else 2
        rs(m, p, direction, at(s, mod(z + (1 - 2 * direction) * step, nz), x)).start()
        rs_pieces.append(4 if whole(m) else 1)

    def fin_piece(i, xp):
        d = mod(xp - x, NX)
        src = fin_s.at[i, pl.ds(pl.multiple_of(32 * xp, 32), 32)]
        c = remote(src, fin_r.at[i, d], finr.at[d], at(s, mod(z + DELTAS[i], nz), xp), 1)
        c.start()
        rs_pieces.append(1)

    def fin_start(i):
        for d in range(NX):
            if (DELTAS[i], d) != (0, 0):
                fin_piece(i, mod(x + d, NX))

    def own(m, direction):
        return partial(mod(z + (1 - 2 * direction) * m, nz))

    def leaf(m):
        for direction in range(2):
            value = own(m, direction).astype(BF16)
            if m == 1:
                fin_s[2 + direction] = value
                fin_start(2 + direction)
                continue
            rs_s[direction, m] = value
            for p in range(1 if whole(m) else NX):
                if m < half or p // 2 == direction:
                    rs_start(m, p, direction)

    leaf(half)
    leaf(half - 1)
    sq = []
    for d in range(1, nz):
        c = remote(sqs, sqr.at[d - 1], sqrs.at[0], at(s, mod(z + d, nz), x), 9)
        c.start()
        sq.append(c)
    leaf(half - 3)

    mine = partial(z)
    fin_s[4] = mine.astype(BF16)
    sqt_sends = []
    for m in range(half - 2, 0, -2):
        values = [own(m, direction) for direction in range(2)]
        for p in range(NX):
            part = slice(32 * p, 32 * p + 32)
            for direction in range(2):
                if p == 0 and whole(m + 1):
                    rs(m + 1, p, direction, x_up).wait_recv()
                two = m + 2 < half or p // 2 == direction
                both = two and not whole(m + 1)
                if two or not whole(m + 1):
                    wait_in(tok.at[pl.ds(0, 64 if both else 32)], rsr.at[direction, m // 2, p])
                value = values[direction][part] + rs_r[direction, m + 1, part, :].astype(F32)
                if two:
                    value = value + rs_r[direction, m + 2, part, :].astype(F32)
                if m > 2:
                    rs_s[direction, m, part, :] = value.astype(BF16)
                    rs_start(m, p, direction)
                else:
                    fin_s[direction, part, :] = value.astype(BF16)
                    fin_piece(direction, p)
        if m > 3:
            leaf(m - 3)
        if m == half - 2:
            fin_start(4)
            total_sq = sqs[...]
            wait_in(sqr, sqrs.at[0])
            for d in range(1, nz):
                total_sq = total_sq + sqr[d - 1]
            sqt[...] = total_sq
            for d in range(1, NX):
                c = remote(sqt, sqx.at[d - 1], sqtr.at[0], at(s, z, mod(x + d, NX)), 10)
                c.start()
                sqt_sends.append(c)

    wait_in(sqx, sqtr.at[0])
    for d in range(NX):
        if d > 0:
            squares = sqx[d - 1]
        else:
            squares = sqt[...]
        scale = lax.rsqrt(squares / (BLK * nz) + 1e-05)
        if d == 0:
            total = fin_s[4, pl.ds(pl.multiple_of(32 * x, 32), 32), :].astype(F32)
        wait_in(tok.at[pl.ds(0, 160 if d else 128)], finr.at[d])
        for i in (4, 2, 3, 0, 1):
            if (DELTAS[i], d) != (0, 0):
                got = fin_r[i, d].astype(F32)
                total = got if i == 4 else total + got
        from_x = mod(x - d, NX)
        out_ref[:, pl.ds(pl.multiple_of(BLK * from_x, BLK), BLK)] = (total * scale).astype(BF16)

    wait_out(tok.at[pl.ds(0, 32 * (len(first_sends) + sum(ag_pieces)))], 0)
    wait_out(tok.at[pl.ds(0, 32 * sum(rs_pieces))], 1)
    wait_out(zw.at[pl.ds(0, 192)], 2)
    wait_out(zw.at[pl.ds(0, 192)], 3)
    wait_out(ow.at[pl.ds(0, 192)], 4)
    wait_out(par.at[pl.ds(0, NX - 1)], 5)
    wait_out(halo_s, 6)
    wait_out(st1s.at[pl.ds(0, NX - 1)], 7)
    wait_out(hs.at[pl.ds(0, NX - 1)], 8)
    wait_out(sqr, 9)
    wait_out(sqx, 10)
    for t in range(1, ns):

        @pl.when(s + t < ns)
        def _():
            s2(t).wait_send()


def solution(mesh):
    ns = mesh.shape["seq"]
    nz = mesh.shape["head"] // NX
    half = nz // 2

    def body(tokens, z_weight, x_weight, bc_weight, step_weight, x_kernel, bc_kernel, step_bias, log_decay, skip_gain, norm_gain, out_weight):
        width = bc_weight.shape[0]
        vmem = pl.BlockSpec(memory_space=pltpu.VMEM)
        hbm = pl.BlockSpec(memory_space=pltpu.HBM)
        smem = pl.BlockSpec(memory_space=pltpu.SMEM)
        dma = pltpu.SemaphoreType.DMA

        def pin(value):
            return pltpu.with_memory_space_constraint(value, pltpu.HBM)

        def buf(*shape, dtype=BF16):
            return pltpu.VMEM(shape, dtype)

        out = pl.pallas_call(
            functools.partial(kernel, ns, nz),
            out_shape=pltpu.VMEM((32, 4 * BLK), BF16),
            in_specs=[hbm, hbm, hbm, hbm, vmem, vmem, vmem, smem, smem, smem, vmem, hbm],
            out_specs=vmem,
            scratch_shapes=[
                buf(width, BLK),
                buf(256, width),
                buf(256, width),
                buf(width, 256),
                buf(256, width),
                buf(256, width),
                buf(width, 256),
                buf(NX, 24, 128, dtype=F32),
                buf(8, width, dtype=F32),
                buf(128, 512, dtype=F32),
                buf(512, 128, dtype=F32),
                buf(128, 512, dtype=F32),
                buf(512, BLK),
                buf(256, BLK, dtype=F32),
                buf(256, BLK),
                buf(16, 512),
                buf(16, 512),
                buf(128, BLK, dtype=F32),
                buf(512, BLK, dtype=F32),
                buf(256, BLK),
                buf(256, BLK, dtype=F32),
                buf(NX, 72, 128, dtype=F32),
                buf(NX, 72, 128, dtype=F32),
                buf(72, 128, dtype=F32),
                buf(ns, 72, 128, dtype=F32),
                buf(NX, 64, 128),
                buf(256, 128),
                buf(1, BLK, dtype=F32),
                buf(nz - 1, 1, BLK, dtype=F32),
                buf(256, BLK),
                buf(1, BLK, dtype=F32),
                buf(NX - 1, 1, BLK, dtype=F32),
                buf(2, half + 1, 128, BLK),
                buf(2, half + 1, 128, BLK),
                buf(5, 128, BLK),
                buf(5, NX, 32, BLK),
                dma((3,)),
                dma((10 + ns,)),
                dma((2, NX)),
                dma((1,)),
                dma((4,)),
                dma((2,)),
                dma((1,)),
                dma((2, half // 2 - 1, NX)),
                dma((2,)),
                dma((1,)),
                dma((1,)),
                dma((ns,)),
                dma((1,)),
                dma((1,)),
                dma((1,)),
                dma((2, half // 2, NX)),
                dma((2, half // 2)),
                dma((NX,)),
            ],
            compiler_params=pltpu.CompilerParams(
                collective_id=0, has_side_effects=True, vmem_limit_bytes=40 * 1024 * 1024
            ),
        )(
            pin(tokens.T),
            pin(z_weight.T),
            pin(x_weight.T),
            pin(bc_weight),
            step_weight.T,
            x_kernel,
            bc_kernel,
            step_bias,
            log_decay,
            skip_gain,
            norm_gain.reshape(1, -1),
            pin(out_weight),
        )
        return out.T

    return jax.shard_map(
        body,
        mesh=mesh,
        in_specs=(
            P("seq", "head"),
            P(None, "head"),
            P(None, "head"),
            P(),
            P(None, "head"),
            P(None, "head"),
            P(),
            P("head"),
            P("head"),
            P("head"),
            P("head"),
            P("head", None),
        ),
        out_specs=P("seq", "head"),
        check_vma=False,
    )
```
